32 devices in a mesh: groups: 2 (over y), seq: 4 (over z), slide: 2 (over x), head: 2 (over core).
Axes of the slice: x: 2, y: 2, z: 4, core: 2. Of those that a mesh axis runs over, the one named last changes fastest.
Arguments:
- latents: bfloat16 [1024, 1024], P(('groups', 'seq'), 'head'), parts along dimension 0, may hold values from -153 to 153
- tile_keys: bfloat16 [4, 1024, 1024], P(('groups', 'slide'), 'seq', 'head'), parts along dimension 0, may hold values from -6 to 6
- tile_values: bfloat16 [4, 1024, 1024], P(('groups', 'slide'), 'seq', 'head'), parts along dimension 0, may hold values from -24 to 24
- tile_mask: int32 [4, 8], P(('groups', 'slide'), 'seq'), parts along dimension 0, may hold values from 0 to 1, as said below
- latent_counts: int32 [4], P(('groups', 'slide')), parts along dimension 0, may hold values from 128 to 512
- out_weight: bfloat16 [1024, 1024], P('head'), may hold values from -0.1875 to 0.1875
- cotangent: bfloat16 [4, 512, 1024], P(('groups', 'slide'), 'seq'), parts along dimension 0, may hold values from -6 to 6
Outputs:
- pooled: bfloat16 [4, 512, 1024], P(('groups', 'slide'), 'seq', 'head'), parts along dimension 0
- grad_latents: float32 [1024, 1024], P(('groups', 'seq'), 'head'), parts along dimension 0
- grad_keys: bfloat16 [4, 1024, 1024], P(('groups', 'slide'), 'seq', 'head'), parts along dimension 0
- grad_values: bfloat16 [4, 1024, 1024], P(('groups', 'slide'), 'seq', 'head'), parts along dimension 0
The draws below stay inside these ranges and needn't reach their ends.
There are 2 independent parts, one for each index of `groups`. The reference program is written for one: setup_inputs(seed, part) draws one part's arguments, and reference() takes and returns one part's arrays. A program takes and returns all parts, laid end to end along the dimension named above; an argument that names none is the same for every part. Nothing has to cross between parts.
Inputs may be any that keep to these rules, and one draw needn't show every extreme that they name: `tile_mask`: every slide has at least one block of 128 tiles marked 1.
All inputs are finite; a program needn't handle non-finite values.
Results may differ from the reference program's by a relative error of at most 0.035.
Values may be sent and summed in bfloat16 or wider, within the bound.
A program may use at most 64 MiB of HBM per device.

```python
import jax
import jax.numpy as jnp
from jax import lax

D = 1024
H = 16
HD = 64
LAT = 512
BLOCK = 128
TILES = 1024
SLIDES = 2


def forced_blocks(key):
    return jax.random.randint(jax.random.fold_in(key, 11), (SLIDES,), 0, TILES // BLOCK)


def draw_tile_mask(key, part):
    drawn = jax.random.fold_in(key, 3)
    keep_rates = jax.random.randint(jax.random.fold_in(drawn, 1), (SLIDES, 1), 1, 8)
    block_rolls = jax.random.randint(jax.random.fold_in(drawn, 2), (SLIDES, TILES // BLOCK), 0, 8)
    blocks = (block_rolls < keep_rates).astype(jnp.int32)
    block_ids = jnp.arange(TILES // BLOCK)[None, :]
    forced_ids = forced_blocks(key)
    return jnp.where(block_ids == forced_ids[:, None], 1, blocks).astype(jnp.int32)


def draw_tile_keys(key, part):
    drawn = jax.random.normal(jax.random.fold_in(key, 5), (SLIDES, TILES, D), jnp.float32)
    return jnp.clip(drawn, -6.0, 6.0).astype(jnp.bfloat16)


def draw_latents(key, part):
    drawn = jax.random.normal(jax.random.fold_in(key, 9), (LAT, D), jnp.float32) * 2.5
    return jnp.clip(drawn, -15.0, 15.0).astype(jnp.bfloat16)


def levels(rng, extent, shards, least, largest):
    factor_of, own = 1.0, jax.random.fold_in(rng, 6)
    for dim, parts in shards:
        steps = jnp.exp(jax.random.uniform(jax.random.fold_in(own, dim), (parts,), jnp.float32, least / len(shards), largest / len(shards)))
        factor_of = factor_of * jnp.repeat(steps, extent[dim] // parts).reshape([-1 if axis == dim else 1 for axis in range(len(extent))])
    return factor_of


def bell_draw(rng, shape, deviation, bound, cuts=(), dtype=jnp.bfloat16):
    array = deviation * jax.random.normal(rng, shape, jnp.float32)
    if cuts:
        array = array * levels(rng, shape, cuts, -0.22, 0.18)
    return jnp.clip(array, -bound, bound).astype(dtype)


def setup_inputs(seed: int = 0, part: int = 0) -> dict:
    keys = jax.random.split(jax.random.key(seed), 8)
    own_keys = jax.random.split(jax.random.fold_in(keys[7], part), 8)
    return {
        "latents": draw_latents(jax.random.fold_in(jax.random.fold_in(keys[7], part), 71), part),
        "tile_keys": draw_tile_keys(jax.random.fold_in(jax.random.fold_in(keys[7], part), 71), part),
        "tile_values": bell_draw(own_keys[2], (SLIDES, TILES, D), 4.0, 24.0, ((0, 2), (1, 4), (2, 2))),
        "tile_mask": draw_tile_mask(jax.random.fold_in(jax.random.fold_in(keys[7], part), 71), part),
        "latent_counts": jax.random.randint(own_keys[4], (SLIDES,), LAT // 4, LAT + 1).astype(jnp.int32),
        "out_weight": bell_draw(keys[5], (D, D), D ** -0.5, 0.1875, ((0, 2),)),
        "cotangent": bell_draw(own_keys[6], (SLIDES, LAT, D), 1.0, 6.0, ((0, 2), (1, 4))),
    }


masked_score = -1.0e30


def reference(latents, tile_keys, tile_values, tile_mask, latent_counts, out_weight, cotangent):
    factor = HD ** -0.5
    query_heads = latents.reshape(LAT, H, HD).transpose(1, 0, 2)
    row_ids = jnp.arange(LAT).astype(jnp.int32)[:, None]

    def per_slide(inputs):
        key_block, value_block, blocks, live_count, slide_cot = inputs
        valid_tiles = jnp.repeat(blocks > 0, BLOCK)[None, :]
        key_heads = key_block.reshape(TILES, H, HD).transpose(1, 0, 2)
        value_heads = value_block.reshape(TILES, H, HD).transpose(1, 0, 2)

        def scored(query_h, key_h):
            raw_scores = jnp.dot(query_h, key_h.T, preferred_element_type=jnp.float32) * factor
            return jnp.where(valid_tiles, raw_scores, masked_score)

        def forward_head(pieces):
            query_h, key_h, value_h = pieces
            scores = scored(query_h, key_h)
            row_top = jnp.max(scores, axis=1, keepdims=True)
            expos = jnp.where(valid_tiles, jnp.exp(scores - row_top), 0.0)
            row_total = jnp.sum(expos, axis=1, keepdims=True)
            weighted = jnp.dot(expos.astype(jnp.bfloat16), value_h, preferred_element_type=jnp.float32)
            return weighted / row_total, row_top, row_total

        attn_heads, tops, totals = lax.map(forward_head, (query_heads, key_heads, value_heads))
        live = row_ids < live_count
        attended = jnp.where(live, attn_heads.transpose(1, 0, 2).reshape(LAT, D), 0.0).astype(jnp.bfloat16)
        pooled = jnp.dot(attended, out_weight, preferred_element_type=jnp.float32).astype(jnp.bfloat16)
        upstream = jnp.where(live, jnp.dot(slide_cot, out_weight.T, preferred_element_type=jnp.float32), 0.0).astype(jnp.bfloat16)
        up_heads = upstream.reshape(LAT, H, HD).transpose(1, 0, 2)
        att_heads = attended.reshape(LAT, H, HD).transpose(1, 0, 2)

        def backward_head(pieces):
            query_h, key_h, value_h, row_top, row_total, up_h, att_h = pieces
            row_delta = jnp.sum(up_h.astype(jnp.float32) * att_h.astype(jnp.float32), axis=1, keepdims=True)
            scores = scored(query_h, key_h)
            weights = jnp.where(valid_tiles, jnp.exp(scores - row_top), 0.0) / row_total
            grad_value = jnp.dot(weights.astype(jnp.bfloat16).T, up_h, preferred_element_type=jnp.float32)
            grad_prob = jnp.dot(up_h, value_h.T, preferred_element_type=jnp.float32)
            grad_score = (weights * (grad_prob - row_delta) * factor).astype(jnp.bfloat16)
            grad_query = jnp.dot(grad_score, key_h, preferred_element_type=jnp.float32)
            grad_key = jnp.dot(grad_score.T, query_h, preferred_element_type=jnp.float32)
            return grad_query, grad_key, grad_value

        grad_query, grad_key, grad_value = lax.map(backward_head, (query_heads, key_heads, value_heads, tops, totals, up_heads, att_heads))
        grad_query = grad_query.transpose(1, 0, 2).reshape(LAT, D)
        grad_key = grad_key.transpose(1, 0, 2).reshape(TILES, D).astype(jnp.bfloat16)
        grad_value = grad_value.transpose(1, 0, 2).reshape(TILES, D).astype(jnp.bfloat16)
        return pooled, grad_query, grad_key, grad_value

    pooled, grad_query, grad_keys, grad_values = lax.map(per_slide, (tile_keys, tile_values, tile_mask, latent_counts, cotangent))
    return pooled, jnp.sum(grad_query, axis=0), grad_keys, grad_values
```

```python
import functools

import jax
import jax.numpy as jnp
from jax import lax
from jax.experimental import pallas as pl
from jax.experimental.pallas import tpu as pltpu
from jax.sharding import PartitionSpec as P

HD = 64
BLOCK = 128


masked_score = -1e30


MESH = pl.DeviceIdType.MESH


def dot(a, b, dims):
    return lax.dot_general(a, b, (dims, ((), ())), preferred_element_type=jnp.float32)


def swap_kernel(
    n,
    slides,
    latents,
    keys,
    values,
    mask,
    count,
    weight,
    cot,
    pooled,
    grad_latents,
    grad_keys,
    grad_values,
    q_all,
    k_all,
    v_all,
    u_all,
    mask_own,
    mask_all,
    w_buf,
    cot_buf,
    u_own,
    probs,
    att,
    att_in,
    part_out,
    part_in,
    gk,
    gv,
    gq,
    gq_in,
    gq_sum,
    gl_in,
    local_sem,
    send_sem,
    recv_sem,
    slide_send,
    slide_recv,
    head_send,
    head_recv,
):
    me = lax.axis_index("seq")
    my_head = lax.axis_index("head")
    my_slide = lax.axis_index("slide")
    rows = latents.shape[0]
    tiles = keys.shape[1]
    blk = q_all.shape[1]
    heads = blk // HD
    width = latents.shape[1]
    all_rows = n * rows
    blocks = tiles // BLOCK
    factor = HD ** (-0.5)

    def cols(j):
        return pl.ds(pl.multiple_of(j * blk, 128), blk)

    def rows_of(j, size):
        return pl.ds(pl.multiple_of(j * size, 128), size)

    def peer(d):
        return lax.rem(me + d, n)

    barrier = pltpu.get_barrier_semaphore()
    for d in range(1, n):
        pl.semaphore_signal(barrier, inc=1, device_id={"seq": peer(d)}, device_id_type=MESH)
    for e in range(1, slides):
        other = lax.rem(my_slide + e, slides)
        pl.semaphore_signal(barrier, inc=1, device_id={"slide": other}, device_id_type=MESH)
    pl.semaphore_signal(barrier, inc=1, device_id={"head": 1 - my_head}, device_id_type=MESH)

    def local(src, dst, i):
        copy = pltpu.make_async_copy(src, dst, local_sem.at[i])
        copy.start()
        return copy

    w_copy = local(weight, w_buf, 0)
    cot_copy = local(cot.at[0], cot_buf, 1)
    own_q = local(latents.at[:, cols(me)], q_all.at[rows_of(me, rows)], 2)
    own_k = local(keys.at[0, :, cols(me)], k_all.at[rows_of(me, tiles)], 3)
    own_v = local(values.at[0, :, cols(me)], v_all.at[rows_of(me, tiles)], 4)
    mask_own[...] = jnp.zeros_like(mask_own)
    for b in range(blocks):
        mask_own[pl.ds(b, 1), :] = jnp.full((1, 128), mask[0, b], jnp.int32)
    mask_all[me] = mask_own[...]

    sent = []

    def send(kind, d, src, dst):
        copy = pltpu.make_async_remote_copy(
            src_ref=src,
            dst_ref=dst,
            send_sem=send_sem.at[kind, d - 1],
            recv_sem=recv_sem.at[kind, d - 1],
            device_id={"seq": peer(d)},
            device_id_type=MESH,
        )
        copy.start()
        sent.append(copy)
        return copy

    far = list(range(1, n))
    pl.semaphore_wait(barrier, n - 1 + slides - 1 + 1)
    mask_moves = [send(0, d, mask_own, mask_all.at[me]) for d in far]
    q_moves = [send(1, d, latents.at[:, cols(peer(d))], q_all.at[rows_of(me, rows)]) for d in far]
    k_moves = [send(2, d, keys.at[0, :, cols(peer(d))], k_all.at[rows_of(me, tiles)]) for d in far]
    v_moves = [send(3, d, values.at[0, :, cols(peer(d))], v_all.at[rows_of(me, tiles)]) for d in far]

    live_count = count[0]
    w_copy.wait()
    cot_copy.wait()
    own_row = lax.broadcasted_iota(jnp.int32, (rows, 1), 0) + me * rows
    for j in range(n):
        projected = dot(cot_buf[...], w_buf[j * blk : (j + 1) * blk, :], ((1,), (1,)))
        u_own[:, j * blk : (j + 1) * blk] = jnp.where(own_row < live_count, projected, 0.0).astype(
            jnp.bfloat16
        )
    own_u = local(u_own.at[:, cols(me)], u_all.at[rows_of(me, rows)], 5)
    u_moves = [send(4, d, u_own.at[:, cols(peer(d))], u_all.at[rows_of(me, rows)]) for d in far]

    lane = lax.broadcasted_iota(jnp.int32, (1, blk), 1) // HD

    def only(x, h):
        return jnp.where(lane == h, x, jnp.zeros_like(x))

    own_q.wait()
    own_k.wait()
    for copy in mask_moves + q_moves + k_moves:
        copy.wait_recv()

    tops = []
    totals = []
    for h in range(heads):
        query = only(q_all[...], h)

        def score_step(i, top, h=h, query=query):
            for b in range(blocks):
                at = pl.ds(pl.multiple_of(i * tiles + b * BLOCK, BLOCK), BLOCK)
                score = dot(k_all[at, :], query, ((1,), (1,))) * factor
                valid = jnp.broadcast_to(mask_all[i][b : b + 1, :1], (1, all_rows)) > 0
                score = jnp.where(valid, score, masked_score)
                probs[h, at, :] = score
                top = jnp.maximum(top, jnp.max(score, axis=0, keepdims=True))
            return top

        top = lax.fori_loop(0, n, score_step, jnp.full((1, all_rows), masked_score, jnp.float32))

        def exp_step(i, total, h=h, top=top):
            for b in range(blocks):
                at = pl.ds(pl.multiple_of(i * tiles + b * BLOCK, BLOCK), BLOCK)
                expos = jnp.exp(probs[h, at, :] - top)
                probs[h, at, :] = expos
                total = total + jnp.sum(expos, axis=0, keepdims=True)
            return total

        totals.append(lax.fori_loop(0, n, exp_step, jnp.zeros((1, all_rows), jnp.float32)))
    inverse = [1.0 / total for total in totals]

    own_v.wait()
    for copy in v_moves:
        copy.wait_recv()

    def attend_step(i, sums):
        at = rows_of(i, tiles)
        v_block = v_all[at, :]
        return tuple(
            sums[h] + dot(only(v_block, h), probs[h, at, :].astype(jnp.bfloat16), ((0,), (0,)))
            for h in range(heads)
        )

    zero = jnp.zeros((blk, all_rows), jnp.float32)
    sums = lax.fori_loop(0, n, attend_step, (zero,) * heads)
    attended = sums[0] * inverse[0]
    for h in range(1, heads):
        attended = attended + sums[h] * inverse[h]
    every_row = lax.broadcasted_iota(jnp.int32, (1, all_rows), 1)
    attended = jnp.where(every_row < live_count, attended, 0.0)
    attended_rows = attended.T.astype(jnp.bfloat16)
    att[...] = attended_rows
    own_att = local(att.at[rows_of(me, rows)], att_in.at[:, cols(me)], 6)
    att_moves = [send(5, d, att.at[rows_of(peer(d), rows)], att_in.at[:, cols(me)]) for d in far]

    own_u.wait()
    for copy in u_moves:
        copy.wait_recv()
    product = u_all[...].astype(jnp.float32) * attended_rows.astype(jnp.float32)
    product = product.T
    delta = [jnp.sum(product[h * HD : (h + 1) * HD], axis=0, keepdims=True) for h in range(heads)]

    grad_q = zero
    gk_moves = []
    gv_moves = []
    for d in far[::-1] + [0]:
        j = peer(d)
        at = rows_of(j, tiles)
        v_block = v_all[at, :]
        k_block = k_all[at, :]
        grad_k = grad_v = None
        for h in range(heads):
            query = only(q_all[...], h)
            up = only(u_all[...], h)
            grad_prob = dot(v_block, up, ((1,), (1,)))
            weights = probs[h, at, :] * inverse[h]
            grad_score = (weights * (grad_prob - delta[h]) * factor).astype(jnp.bfloat16)
            more_v = dot(weights.astype(jnp.bfloat16), up, ((1,), (0,)))
            more_k = dot(grad_score, query, ((1,), (0,)))
            grad_v = more_v if grad_v is None else grad_v + more_v
            grad_k = more_k if grad_k is None else grad_k + more_k
            grad_q = grad_q + dot(only(k_block, h), grad_score, ((0,), (0,)))
        gk[at, :] = grad_k.astype(jnp.bfloat16)
        gv[at, :] = grad_v.astype(jnp.bfloat16)
        if d:
            gk_moves.append(send(6, d, gk.at[at], grad_keys.at[0, :, cols(me)]))
            gv_moves.append(send(7, d, gv.at[at], grad_values.at[0, :, cols(me)]))
        else:
            own_gk = local(gk.at[at], grad_keys.at[0, :, cols(me)], 7)
            own_gv = local(gv.at[at], grad_values.at[0, :, cols(me)], 8)

    grad_rows = grad_q.T
    gq[...] = grad_rows.astype(jnp.bfloat16)
    slide_moves = []
    for e in range(1, slides):
        copy = pltpu.make_async_remote_copy(
            src_ref=gq,
            dst_ref=gq_in.at[e - 1],
            send_sem=slide_send.at[e - 1],
            recv_sem=slide_recv.at[e - 1],
            device_id={"slide": lax.rem(my_slide + e, slides)},
            device_id_type=MESH,
        )
        copy.start()
        slide_moves.append(copy)

    own_att.wait()
    for copy in att_moves:
        copy.wait_recv()
    half = pooled.shape[2]
    mine = pl.ds(pl.multiple_of(my_head * half, 128), half)
    theirs = pl.ds(pl.multiple_of((1 - my_head) * half, 128), half)
    part_out[...] = dot(att_in[...], w_buf[:, theirs], ((1,), (0,))).astype(jnp.bfloat16)
    head_move = pltpu.make_async_remote_copy(
        src_ref=part_out,
        dst_ref=part_in,
        send_sem=head_send,
        recv_sem=head_recv,
        device_id={"head": 1 - my_head},
        device_id_type=MESH,
    )
    head_move.start()
    own_part = dot(att_in[...], w_buf[:, mine], ((1,), (0,)))

    total = grad_rows
    for e, copy in enumerate(slide_moves):
        copy.wait_recv()
        total = total + gq_in[e].astype(jnp.float32)
    gq_sum[...] = total.astype(jnp.bfloat16)
    own_gl = local(gq_sum.at[rows_of(me, rows)], gl_in.at[:, cols(me)], 9)
    gl_moves = [send(8, d, gq_sum.at[rows_of(peer(d), rows)], gl_in.at[:, cols(me)]) for d in far]

    head_move.wait_recv()
    pooled[0] = (own_part + part_in[...].astype(jnp.float32)).astype(jnp.bfloat16)

    own_gl.wait()
    for copy in gl_moves:
        copy.wait_recv()
    grad_latents[...] = gl_in[...].astype(jnp.float32)
    own_gk.wait()
    own_gv.wait()
    for copy in gk_moves + gv_moves:
        copy.wait_recv()
    for copy in sent + slide_moves + [head_move]:
        copy.wait_send()


def swapped_body(latents, tile_keys, tile_values, tile_mask, latent_counts, out_weight, cotangent):
    n = lax.axis_size("seq")
    slides = lax.axis_size("slide")
    rows, width = latents.shape
    tiles = tile_keys.shape[1]
    depth = out_weight.shape[1]
    blk = width // n
    heads = blk // HD
    half = depth // 2
    bf16 = jnp.bfloat16
    anywhere = pl.BlockSpec(memory_space=pl.ANY)
    scalars = pl.BlockSpec(memory_space=pltpu.SMEM)
    vmem = pl.BlockSpec(memory_space=pltpu.VMEM)
    dma = pltpu.SemaphoreType.DMA
    flops = 2 * heads * 6 * n * rows * n * tiles * HD + 4 * rows * width * depth
    return pl.pallas_call(
        functools.partial(swap_kernel, n, slides),
        out_shape=(
            jax.ShapeDtypeStruct((1, rows, half), bf16),
            jax.ShapeDtypeStruct((rows, width), jnp.float32),
            jax.ShapeDtypeStruct(tile_keys.shape, bf16),
            jax.ShapeDtypeStruct(tile_values.shape, bf16),
        ),
        in_specs=[anywhere, anywhere, anywhere, scalars, scalars, anywhere, anywhere],
        out_specs=(vmem, vmem, anywhere, anywhere),
        scratch_shapes=[
            pltpu.VMEM((n * rows, blk), bf16),
            pltpu.VMEM((n * tiles, blk), bf16),
            pltpu.VMEM((n * tiles, blk), bf16),
            pltpu.VMEM((n * rows, blk), bf16),
            pltpu.VMEM((8 * pl.cdiv(tiles // BLOCK, 8), 128), jnp.int32),
            pltpu.VMEM((n, 8 * pl.cdiv(tiles // BLOCK, 8), 128), jnp.int32),
            pltpu.VMEM((width, depth), bf16),
            pltpu.VMEM((rows, depth), bf16),
            pltpu.VMEM((rows, width), bf16),
            pltpu.VMEM((heads, n * tiles, n * rows), jnp.float32),
            pltpu.VMEM((n * rows, blk), bf16),
            pltpu.VMEM((rows, width), bf16),
            pltpu.VMEM((rows, half), bf16),
            pltpu.VMEM((rows, half), bf16),
            pltpu.VMEM((n * tiles, blk), bf16),
            pltpu.VMEM((n * tiles, blk), bf16),
            pltpu.VMEM((n * rows, blk), bf16),
            pltpu.VMEM((slides - 1, n * rows, blk), bf16),
            pltpu.VMEM((n * rows, blk), bf16),
            pltpu.VMEM((rows, width), bf16),
            dma((10,)),
            dma((9, n - 1)),
            dma((9, n - 1)),
            dma((slides - 1,)),
            dma((slides - 1,)),
            dma,
            dma,
        ],
        compiler_params=pltpu.CompilerParams(
            collective_id=0, has_side_effects=True, vmem_limit_bytes=40 * 1024 * 1024
        ),
        cost_estimate=pl.CostEstimate(
            flops=flops, bytes_accessed=8 * rows * depth * 2, transcendentals=heads * n * rows * n * tiles
        ),
    )(latents, tile_keys, tile_values, tile_mask, latent_counts, out_weight, cotangent)


def body(latents, tile_keys, tile_values, tile_mask, latent_counts, out_weight, cotangent):
    local_rows = latents.shape[0]
    local_width = latents.shape[1]
    head_count = local_width // HD
    factor = HD ** (-0.5)
    queries = lax.all_gather(latents, "seq", axis=0, tiled=True)
    total_rows = queries.shape[0]
    first_row = lax.axis_index("seq") * local_rows
    every_row = lax.broadcasted_iota(jnp.int32, (total_rows, 1), 0)
    own_row = lax.broadcasted_iota(jnp.int32, (local_rows, 1), 0) + first_row
    tile_count = tile_keys.shape[1]
    key_block = tile_keys[0]
    value_block = tile_values[0]
    valid_tiles = jnp.broadcast_to(tile_mask[0][:, None] > 0, (tile_count // BLOCK, BLOCK)).reshape(
        1, tile_count
    )
    live_count = latent_counts[0]
    score_list = []
    for which_head in range(head_count):
        columns = slice(which_head * HD, (which_head + 1) * HD)
        raw_scores = (
            jnp.einsum(
                "qc,tc->qt",
                queries[:, columns],
                key_block[:, columns],
                preferred_element_type=jnp.float32,
            )
            * factor
        )
        score_list.append(jnp.where(valid_tiles, raw_scores, masked_score))
    local_top = jnp.stack([jnp.max(scored, axis=1) for scored in score_list], axis=1)
    row_top = lax.pmax(local_top, "seq")
    expo_list = []
    weighted_list = []
    total_list = []
    for which_head in range(head_count):
        columns = slice(which_head * HD, (which_head + 1) * HD)
        expos = jnp.where(
            valid_tiles,
            jnp.exp(score_list[which_head] - row_top[:, which_head : which_head + 1]),
            0.0,
        )
        expo_list.append(expos)
        total_list.append(jnp.sum(expos, axis=1))
        weighted_list.append(
            jnp.dot(
                expos.astype(jnp.bfloat16),
                value_block[:, columns],
                preferred_element_type=jnp.float32,
            )
        )
    partial_sums = jnp.concatenate(weighted_list, axis=1)
    partial_totals = jnp.stack(total_list, axis=1)
    weighted, totals = lax.psum((partial_sums, partial_totals), "seq")
    span = weighted.shape[0]
    attended = jnp.where(
        every_row < live_count,
        (weighted.reshape(span, head_count, HD) / totals[:, :, None]).reshape(span, local_width),
        0.0,
    ).astype(jnp.bfloat16)
    own_attended = lax.dynamic_slice_in_dim(attended, first_row, local_rows, 0)
    pooled_part = jnp.dot(own_attended, out_weight, preferred_element_type=jnp.float32)
    pooled_parts = [
        lax.psum_scatter(pooled_part.astype(jnp.bfloat16), "head", scatter_dimension=1, tiled=True)
    ]
    projected = jnp.einsum(
        "rd,cd->rc", cotangent[0], out_weight, preferred_element_type=jnp.float32
    )
    upstream = jnp.where(own_row < live_count, projected, 0.0).astype(jnp.bfloat16)
    upstream_all = lax.all_gather(upstream, "seq", axis=0, tiled=True)
    row_delta = jnp.sum(
        (upstream_all.astype(jnp.float32) * attended.astype(jnp.float32)).reshape(
            total_rows, head_count, HD
        ),
        axis=2,
    )
    query_list = []
    key_list = []
    value_list = []
    for which_head in range(head_count):
        columns = slice(which_head * HD, (which_head + 1) * HD)
        up_head = upstream_all[:, columns]
        weights = expo_list[which_head] / totals[:, which_head : which_head + 1]
        value_list.append(
            jnp.einsum(
                "qt,qc->tc",
                weights.astype(jnp.bfloat16),
                up_head,
                preferred_element_type=jnp.float32,
            )
        )
        grad_prob = jnp.einsum(
            "qc,tc->qt", up_head, value_block[:, columns], preferred_element_type=jnp.float32
        )
        grad_score = (
            weights * (grad_prob - row_delta[:, which_head : which_head + 1]) * factor
        ).astype(jnp.bfloat16)
        query_list.append(
            jnp.dot(grad_score, key_block[:, columns], preferred_element_type=jnp.float32)
        )
        key_list.append(
            jnp.einsum(
                "qt,qc->tc", grad_score, queries[:, columns], preferred_element_type=jnp.float32
            )
        )
    grad_rows = jnp.concatenate(query_list, axis=1)
    key_grads = [jnp.concatenate(key_list, axis=1).astype(jnp.bfloat16)]
    value_grads = [jnp.concatenate(value_list, axis=1).astype(jnp.bfloat16)]
    own_grad = lax.psum_scatter(
        grad_rows.astype(jnp.bfloat16), "seq", scatter_dimension=0, tiled=True
    )
    grad_latents = lax.psum(own_grad, "slide").astype(jnp.float32)
    return (
        jnp.stack(pooled_parts, axis=0),
        grad_latents,
        jnp.stack(key_grads, axis=0),
        jnp.stack(value_grads, axis=0),
    )


def solution(mesh):
    placed = (
        P(("groups", "seq"), "head"),
        P(("groups", "slide"), "seq", "head"),
        P(("groups", "slide"), "seq", "head"),
        P(("groups", "slide"), "seq"),
        P(("groups", "slide")),
        P("head", None),
        P(("groups", "slide"), "seq", None),
    )
    block_width = 128 * mesh.shape["seq"]
    swapped = mesh.shape["seq"] > 1 and mesh.shape["slide"] > 1 and mesh.shape["head"] == 2

    def chosen(latents, *others):
        by_heads = swapped and latents.shape[1] % block_width == 0
        by_heads = by_heads and latents.shape[0] % 128 == 0 and others[0].shape[1] % BLOCK == 0
        return (swapped_body if by_heads else body)(latents, *others)

    return jax.shard_map(
        chosen,
        mesh=mesh,
        in_specs=placed,
        out_specs=(
            P(("groups", "slide"), "seq", "head"),
            P(("groups", "seq"), "head"),
            P(("groups", "slide"), "seq", "head"),
            P(("groups", "slide"), "seq", "head"),
        ),
        check_vma=False,
    )
```

```python
import functools

import jax
import jax.numpy as jnp
from jax import lax
from jax.experimental import pallas as pl
from jax.experimental.pallas import tpu as pltpu
from jax.sharding import PartitionSpec as P

HD = 64
BLOCK = 128


masked_score = -1e30


MESH = pl.DeviceIdType.MESH


def dot(a, b, dims):
    return lax.dot_general(a, b, (dims, ((), ())), preferred_element_type=jnp.float32)


def swap_kernel(
    n,
    slides,
    latents,
    keys,
    values,
    mask,
    count,
    weight,
    cot,
    pooled,
    grad_latents,
    grad_keys,
    grad_values,
    q_all,
    k_all,
    v_all,
    u_all,
    mask_own,
    mask_all,
    w_buf,
    cot_buf,
    u_own,
    probs,
    att,
    att_in,
    part_out,
    part_in,
    gk,
    gv,
    gq,
    gq_in,
    gq_sum,
    gl_in,
    pooled_buf,
    gl_buf,
    local_sem,
    send_sem,
    recv_sem,
    slide_send,
    slide_recv,
    share_send,
    share_recv,
    head_send,
    head_recv,
):
    me = lax.axis_index("seq")
    my_head = lax.axis_index("head")
    my_slide = lax.axis_index("slide")
    rows = latents.shape[0]
    tiles = keys.shape[1]
    blk = k_all.shape[1]
    share = rows // slides
    heads = blk // HD
    width = latents.shape[1]
    all_rows = n * rows
    blocks = tiles // BLOCK
    factor = HD ** (-0.5)

    def cols(j):
        return pl.ds(pl.multiple_of(j * blk, 128), blk)

    def rows_of(j, size):
        return pl.ds(pl.multiple_of(j * size, 128), size)

    def peer(d):
        other, bit = me, 1
        while bit < n:
            if d & bit:
                other = other + bit - 2 * bit * lax.rem(lax.div(me, bit), 2)
            bit *= 2
        return other

    barrier = pltpu.get_barrier_semaphore()
    for d in range(1, n):
        pl.semaphore_signal(barrier, inc=1, device_id={"seq": peer(d)}, device_id_type=MESH)
    for e in range(1, slides):
        other = lax.rem(my_slide + e, slides)
        pl.semaphore_signal(barrier, inc=1, device_id={"slide": other}, device_id_type=MESH)
    pl.semaphore_signal(barrier, inc=1, device_id={"head": 1 - my_head}, device_id_type=MESH)

    def local(src, dst, i):
        copy = pltpu.make_async_copy(src, dst, local_sem.at[i])
        copy.start()
        return copy

    w_copy = local(weight, w_buf, 0)
    cot_copy = local(cot.at[0], cot_buf, 1)
    my_share = pl.ds(pl.multiple_of(my_slide * share, 16), share)
    own_q = local(latents.at[my_share, cols(me)], q_all.at[me, my_slide], 2)
    own_k = local(keys.at[0, :, cols(me)], k_all.at[rows_of(me, tiles)], 3)
    own_v = local(values.at[0, :, cols(me)], v_all.at[rows_of(me, tiles)], 4)
    mask_own[...] = jnp.zeros_like(mask_own)
    for b in range(blocks):
        mask_own[pl.ds(b, 1), :] = jnp.full((1, 128), mask[0, b], jnp.int32)
    mask_all[me] = mask_own[...]

    sent = []

    def send(kind, d, src, dst):
        copy = pltpu.make_async_remote_copy(
            src_ref=src,
            dst_ref=dst,
            send_sem=send_sem.at[kind, d - 1],
            recv_sem=recv_sem.at[kind, d - 1],
            device_id={"seq": peer(d)},
            device_id_type=MESH,
        )
        copy.start()
        sent.append(copy)
        return copy

    far = [n // 2] + [d for d in range(n - 1, 0, -1) if d != n // 2]
    pl.semaphore_wait(barrier, n - 1 + slides - 1 + 1)
    mask_moves = [send(0, d, mask_own, mask_all.at[me]) for d in far]
    q_moves = [send(1, d, latents.at[my_share, cols(peer(d))], q_all.at[me, my_slide]) for d in far]
    k_moves = [send(2, d, keys.at[0, :, cols(peer(d))], k_all.at[rows_of(me, tiles)]) for d in far]

    live_count = count[0]
    w_copy.wait()
    cot_copy.wait()
    own_row = lax.broadcasted_iota(jnp.int32, (rows, 1), 0) + me * rows
    projected = dot(cot_buf[...], w_buf[...], ((1,), (1,)))
    u_own[...] = jnp.where(own_row < live_count, projected, 0.0).astype(jnp.bfloat16)
    own_u = local(u_own.at[:, cols(me)], u_all.at[rows_of(me, rows)], 5)
    u_moves = [send(4, d, u_own.at[:, cols(peer(d))], u_all.at[rows_of(me, rows)]) for d in far]

    v_moves = [send(3, d, values.at[0, :, cols(peer(d))], v_all.at[rows_of(me, tiles)]) for d in far]

    lane = lax.broadcasted_iota(jnp.int32, (1, blk), 1) // HD

    def only(x, h):
        return jnp.where(lane == h, x, jnp.zeros_like(x))

    own_q.wait()
    for copy in q_moves:
        copy.wait_recv()
    share_moves = []
    for e in range(1, slides):
        copy = pltpu.make_async_remote_copy(
            src_ref=q_all.at[:, my_slide],
            dst_ref=q_all.at[:, my_slide],
            send_sem=share_send.at[e - 1],
            recv_sem=share_recv.at[e - 1],
            device_id={"slide": lax.rem(my_slide + e, slides)},
            device_id_type=MESH,
        )
        copy.start()
        share_moves.append(copy)
    own_k.wait()
    for copy in mask_moves + share_moves + k_moves:
        copy.wait_recv()
    q_rows = q_all[...].reshape(all_rows, blk)

    tops = []
    totals = []
    for h in range(heads):
        query = only(q_rows, h)

        def score_step(i, top, h=h, query=query):
            for b in range(blocks):
                at = pl.ds(pl.multiple_of(i * tiles + b * BLOCK, BLOCK), BLOCK)
                score = dot(k_all[at, :], query, ((1,), (1,))) * factor
                valid = jnp.broadcast_to(mask_all[i][b : b + 1, :1], (1, all_rows)) > 0
                score = jnp.where(valid, score, masked_score)
                probs[h, at, :] = score
                top = jnp.maximum(top, jnp.max(score, axis=0, keepdims=True))
            return top

        top = lax.fori_loop(0, n, score_step, jnp.full((1, all_rows), masked_score, jnp.float32))

        def exp_step(i, total, h=h, top=top):
            for b in range(blocks):
                at = pl.ds(pl.multiple_of(i * tiles + b * BLOCK, BLOCK), BLOCK)
                expos = jnp.exp(probs[h, at, :] - top)
                probs[h, at, :] = expos
                total = total + jnp.sum(expos, axis=0, keepdims=True)
            return total

        totals.append(lax.fori_loop(0, n, exp_step, jnp.zeros((1, all_rows), jnp.float32)))
    inverse = [1.0 / total for total in totals]

    own_u.wait()
    for copy in u_moves:
        copy.wait_recv()
    u_rows = u_all[...]
    gv_moves = []
    for d in far + [0]:
        j = peer(d)
        at = rows_of(j, tiles)
        grad_v = None
        for h in range(heads):
            weights = probs[h, at, :] * inverse[h]
            probs[h, at, :] = weights
            more_v = dot(weights.astype(jnp.bfloat16), only(u_rows, h), ((1,), (0,)))
            grad_v = more_v if grad_v is None else grad_v + more_v
        gv[at, :] = grad_v.astype(jnp.bfloat16)
        if d:
            gv_moves.append(send(7, d, gv.at[at], grad_values.at[0, :, cols(me)]))
        else:
            own_gv = local(gv.at[at], grad_values.at[0, :, cols(me)], 8)

    own_v.wait()
    for copy in v_moves:
        copy.wait_recv()

    def attend_step(i, sums):
        at = rows_of(i, tiles)
        v_block = v_all[at, :]
        for h in range(heads):
            weights = probs[h, at, :].astype(jnp.bfloat16)
            sums = sums + dot(only(v_block, h), weights, ((0,), (0,)))
        return sums

    zero = jnp.zeros((blk, all_rows), jnp.float32)
    attended = lax.fori_loop(0, n, attend_step, zero)
    every_row = lax.broadcasted_iota(jnp.int32, (1, all_rows), 1)
    attended = jnp.where(every_row < live_count, attended, 0.0)
    attended_rows = attended.T.astype(jnp.bfloat16)
    att[...] = attended_rows
    own_att = local(att.at[rows_of(me, rows)], att_in.at[:, cols(me)], 6)
    att_moves = [send(5, d, att.at[rows_of(peer(d), rows)], att_in.at[:, cols(me)]) for d in far]

    product = u_rows.astype(jnp.float32) * attended_rows.astype(jnp.float32)
    product = product.T
    delta = [jnp.sum(product[h * HD : (h + 1) * HD], axis=0, keepdims=True) for h in range(heads)]

    grad_q = zero
    gk_moves = []
    for d in far + [0]:
        j = peer(d)
        at = rows_of(j, tiles)
        v_block = v_all[at, :]
        k_block = k_all[at, :]
        grad_k = None
        for h in range(heads):
            query = only(q_rows, h)
            grad_prob = dot(v_block, only(u_rows, h), ((1,), (1,)))
            weights = probs[h, at, :]
            grad_score = (weights * (grad_prob - delta[h]) * factor).astype(jnp.bfloat16)
            more_k = dot(grad_score, query, ((1,), (0,)))
            grad_k = more_k if grad_k is None else grad_k + more_k
            grad_q = grad_q + dot(only(k_block, h), grad_score, ((0,), (0,)))
        gk[at, :] = grad_k.astype(jnp.bfloat16)
        if d:
            gk_moves.append(send(6, d, gk.at[at], grad_keys.at[0, :, cols(me)]))
        else:
            own_gk = local(gk.at[at], grad_keys.at[0, :, cols(me)], 7)

    grad_rows = grad_q.T
    gq[...] = grad_rows.astype(jnp.bfloat16)
    slide_moves = []
    for e in range(1, slides):
        copy = pltpu.make_async_remote_copy(
            src_ref=gq,
            dst_ref=gq_in.at[e - 1],
            send_sem=slide_send.at[e - 1],
            recv_sem=slide_recv.at[e - 1],
            device_id={"slide": lax.rem(my_slide + e, slides)},
            device_id_type=MESH,
        )
        copy.start()
        slide_moves.append(copy)

    own_att.wait()
    for copy in att_moves:
        copy.wait_recv()
    half = pooled.shape[2]
    mine = pl.ds(pl.multiple_of(my_head * half, 128), half)
    theirs = pl.ds(pl.multiple_of((1 - my_head) * half, 128), half)
    part_out[...] = dot(att_in[...], w_buf[:, theirs], ((1,), (0,))).astype(jnp.bfloat16)
    head_move = pltpu.make_async_remote_copy(
        src_ref=part_out,
        dst_ref=part_in,
        send_sem=head_send,
        recv_sem=head_recv,
        device_id={"head": 1 - my_head},
        device_id_type=MESH,
    )
    head_move.start()
    own_part = dot(att_in[...], w_buf[:, mine], ((1,), (0,)))

    total = grad_rows
    for e, copy in enumerate(slide_moves):
        copy.wait_recv()
        total = total + gq_in[e].astype(jnp.float32)
    gq_sum[...] = total.astype(jnp.bfloat16)
    own_gl = local(gq_sum.at[rows_of(me, rows)], gl_in.at[:, cols(me)], 9)
    gl_moves = [send(8, d, gq_sum.at[rows_of(peer(d), rows)], gl_in.at[:, cols(me)]) for d in far]

    head_move.wait_recv()
    pooled_buf[...] = (own_part + part_in[...].astype(jnp.float32)).astype(jnp.bfloat16)

    out_pooled = local(pooled_buf, pooled.at[0], 10)
    own_gl.wait()
    for copy in gl_moves:
        copy.wait_recv()
    gl_buf[...] = gl_in[...].astype(jnp.float32)
    out_gl = local(gl_buf, grad_latents, 11)
    own_gk.wait()
    own_gv.wait()
    for copy in gk_moves + gv_moves:
        copy.wait_recv()
    for copy in sent + slide_moves + share_moves + [head_move]:
        copy.wait_send()
    out_pooled.wait()
    out_gl.wait()


def finish_kernel(count, *refs):
    sems = refs[-1]
    copies = [pltpu.make_async_copy(refs[i], refs[count + i], sems.at[i]) for i in range(count)]
    for copy in copies:
        copy.start()
    for copy in copies:
        copy.wait()


def swapped_body(latents, tile_keys, tile_values, tile_mask, latent_counts, out_weight, cotangent):
    n = lax.axis_size("seq")
    slides = lax.axis_size("slide")
    rows, width = latents.shape
    tiles = tile_keys.shape[1]
    depth = out_weight.shape[1]
    blk = width // n
    heads = blk // HD
    half = depth // 2
    bf16 = jnp.bfloat16
    anywhere = pl.BlockSpec(memory_space=pltpu.HBM)
    scalars = pl.BlockSpec(memory_space=pltpu.SMEM)
    dma = pltpu.SemaphoreType.DMA
    flops = 2 * heads * 6 * n * rows * n * tiles * HD + 4 * rows * width * depth
    results = pl.pallas_call(
        functools.partial(swap_kernel, n, slides),
        out_shape=(
            jax.ShapeDtypeStruct((1, rows, half), bf16),
            jax.ShapeDtypeStruct((rows, width), jnp.float32),
            jax.ShapeDtypeStruct(tile_keys.shape, bf16),
            jax.ShapeDtypeStruct(tile_values.shape, bf16),
        ),
        in_specs=[anywhere, anywhere, anywhere, scalars, scalars, anywhere, anywhere],
        out_specs=(anywhere,) * 4,
        scratch_shapes=[
            pltpu.VMEM((n, slides, rows // slides, blk), bf16),
            pltpu.VMEM((n * tiles, blk), bf16),
            pltpu.VMEM((n * tiles, blk), bf16),
            pltpu.VMEM((n * rows, blk), bf16),
            pltpu.VMEM((8 * pl.cdiv(tiles // BLOCK, 8), 128), jnp.int32),
            pltpu.VMEM((n, 8 * pl.cdiv(tiles // BLOCK, 8), 128), jnp.int32),
            pltpu.VMEM((width, depth), bf16),
            pltpu.VMEM((rows, depth), bf16),
            pltpu.VMEM((rows, width), bf16),
            pltpu.VMEM((heads, n * tiles, n * rows), jnp.float32),
            pltpu.VMEM((n * rows, blk), bf16),
            pltpu.VMEM((rows, width), bf16),
            pltpu.VMEM((rows, half), bf16),
            pltpu.VMEM((rows, half), bf16),
            pltpu.VMEM((n * tiles, blk), bf16),
            pltpu.VMEM((n * tiles, blk), bf16),
            pltpu.VMEM((n * rows, blk), bf16),
            pltpu.VMEM((slides - 1, n * rows, blk), bf16),
            pltpu.VMEM((n * rows, blk), bf16),
            pltpu.VMEM((rows, width), bf16),
            pltpu.VMEM((rows, half), bf16),
            pltpu.VMEM((rows, width), jnp.float32),
            dma((12,)),
            dma((9, n - 1)),
            dma((9, n - 1)),
            dma((slides - 1,)),
            dma((slides - 1,)),
            dma((slides - 1,)),
            dma((slides - 1,)),
            dma,
            dma,
        ],
        compiler_params=pltpu.CompilerParams(
            collective_id=0, has_side_effects=True, vmem_limit_bytes=60 * 1024 * 1024
        ),
        cost_estimate=pl.CostEstimate(
            flops=flops, bytes_accessed=8 * rows * depth * 2, transcendentals=heads * n * rows * n * tiles
        ),
    )(latents, tile_keys, tile_values, tile_mask, latent_counts, out_weight, cotangent)
    return pl.pallas_call(
        functools.partial(finish_kernel, len(results)),
        out_shape=tuple(jax.ShapeDtypeStruct(x.shape, x.dtype) for x in results),
        in_specs=[anywhere] * len(results),
        out_specs=(anywhere,) * len(results),
        scratch_shapes=[dma((len(results),))],
        compiler_params=pltpu.CompilerParams(vmem_limit_bytes=60 * 1024 * 1024),
    )(*results)


def body(latents, tile_keys, tile_values, tile_mask, latent_counts, out_weight, cotangent):
    local_rows = latents.shape[0]
    local_width = latents.shape[1]
    head_count = local_width // HD
    factor = HD ** (-0.5)
    queries = lax.all_gather(latents, "seq", axis=0, tiled=True)
    total_rows = queries.shape[0]
    first_row = lax.axis_index("seq") * local_rows
    every_row = lax.broadcasted_iota(jnp.int32, (total_rows, 1), 0)
    own_row = lax.broadcasted_iota(jnp.int32, (local_rows, 1), 0) + first_row
    tile_count = tile_keys.shape[1]
    key_block = tile_keys[0]
    value_block = tile_values[0]
    valid_tiles = jnp.broadcast_to(tile_mask[0][:, None] > 0, (tile_count // BLOCK, BLOCK)).reshape(
        1, tile_count
    )
    live_count = latent_counts[0]
    score_list = []
    for which_head in range(head_count):
        columns = slice(which_head * HD, (which_head + 1) * HD)
        raw_scores = (
            jnp.einsum(
                "qc,tc->qt",
                queries[:, columns],
                key_block[:, columns],
                preferred_element_type=jnp.float32,
            )
            * factor
        )
        score_list.append(jnp.where(valid_tiles, raw_scores, masked_score))
    local_top = jnp.stack([jnp.max(scored, axis=1) for scored in score_list], axis=1)
    row_top = lax.pmax(local_top, "seq")
    expo_list = []
    weighted_list = []
    total_list = []
    for which_head in range(head_count):
        columns = slice(which_head * HD, (which_head + 1) * HD)
        expos = jnp.where(
            valid_tiles,
            jnp.exp(score_list[which_head] - row_top[:, which_head : which_head + 1]),
            0.0,
        )
        expo_list.append(expos)
        total_list.append(jnp.sum(expos, axis=1))
        weighted_list.append(
            jnp.dot(
                expos.astype(jnp.bfloat16),
                value_block[:, columns],
                preferred_element_type=jnp.float32,
            )
        )
    partial_sums = jnp.concatenate(weighted_list, axis=1)
    partial_totals = jnp.stack(total_list, axis=1)
    weighted, totals = lax.psum((partial_sums, partial_totals), "seq")
    span = weighted.shape[0]
    attended = jnp.where(
        every_row < live_count,
        (weighted.reshape(span, head_count, HD) / totals[:, :, None]).reshape(span, local_width),
        0.0,
    ).astype(jnp.bfloat16)
    own_attended = lax.dynamic_slice_in_dim(attended, first_row, local_rows, 0)
    pooled_part = jnp.dot(own_attended, out_weight, preferred_element_type=jnp.float32)
    pooled_parts = [
        lax.psum_scatter(pooled_part.astype(jnp.bfloat16), "head", scatter_dimension=1, tiled=True)
    ]
    projected = jnp.einsum(
        "rd,cd->rc", cotangent[0], out_weight, preferred_element_type=jnp.float32
    )
    upstream = jnp.where(own_row < live_count, projected, 0.0).astype(jnp.bfloat16)
    upstream_all = lax.all_gather(upstream, "seq", axis=0, tiled=True)
    row_delta = jnp.sum(
        (upstream_all.astype(jnp.float32) * attended.astype(jnp.float32)).reshape(
            total_rows, head_count, HD
        ),
        axis=2,
    )
    query_list = []
    key_list = []
    value_list = []
    for which_head in range(head_count):
        columns = slice(which_head * HD, (which_head + 1) * HD)
        up_head = upstream_all[:, columns]
        weights = expo_list[which_head] / totals[:, which_head : which_head + 1]
        value_list.append(
            jnp.einsum(
                "qt,qc->tc",
                weights.astype(jnp.bfloat16),
                up_head,
                preferred_element_type=jnp.float32,
            )
        )
        grad_prob = jnp.einsum(
            "qc,tc->qt", up_head, value_block[:, columns], preferred_element_type=jnp.float32
        )
        grad_score = (
            weights * (grad_prob - row_delta[:, which_head : which_head + 1]) * factor
        ).astype(jnp.bfloat16)
        query_list.append(
            jnp.dot(grad_score, key_block[:, columns], preferred_element_type=jnp.float32)
        )
        key_list.append(
            jnp.einsum(
                "qt,qc->tc", grad_score, queries[:, columns], preferred_element_type=jnp.float32
            )
        )
    grad_rows = jnp.concatenate(query_list, axis=1)
    key_grads = [jnp.concatenate(key_list, axis=1).astype(jnp.bfloat16)]
    value_grads = [jnp.concatenate(value_list, axis=1).astype(jnp.bfloat16)]
    own_grad = lax.psum_scatter(
        grad_rows.astype(jnp.bfloat16), "seq", scatter_dimension=0, tiled=True
    )
    grad_latents = lax.psum(own_grad, "slide").astype(jnp.float32)
    return (
        jnp.stack(pooled_parts, axis=0),
        grad_latents,
        jnp.stack(key_grads, axis=0),
        jnp.stack(value_grads, axis=0),
    )


def solution(mesh):
    placed = (
        P(("groups", "seq"), "head"),
        P(("groups", "slide"), "seq", "head"),
        P(("groups", "slide"), "seq", "head"),
        P(("groups", "slide"), "seq"),
        P(("groups", "slide")),
        P("head", None),
        P(("groups", "slide"), "seq", None),
    )
    block_width = 128 * mesh.shape["seq"]
    swapped = mesh.shape["seq"] in (2, 4, 8) and mesh.shape["slide"] > 1 and mesh.shape["head"] == 2

    def chosen(latents, *others):
        by_heads = swapped and latents.shape[1] % block_width == 0
        by_heads = by_heads and latents.shape[0] % 128 == 0
        by_heads = by_heads and latents.shape[0] % (16 * mesh.shape["slide"]) == 0 and others[0].shape[1] % BLOCK == 0
        return (swapped_body if by_heads else body)(latents, *others)

    return jax.shard_map(
        chosen,
        mesh=mesh,
        in_specs=placed,
        out_specs=(
            P(("groups", "slide"), "seq", "head"),
            P(("groups", "seq"), "head"),
            P(("groups", "slide"), "seq", "head"),
            P(("groups", "slide"), "seq", "head"),
        ),
        check_vma=False,
    )
```

```python
import functools

import jax
import jax.numpy as jnp
from jax import lax
from jax.experimental import pallas as pl
from jax.experimental.pallas import tpu as pltpu
from jax.sharding import PartitionSpec as P

HD = 64
BLOCK = 128


masked_score = -1e30


MESH = pl.DeviceIdType.MESH


def dot(a, b, dims):
    return lax.dot_general(a, b, (dims, ((), ())), preferred_element_type=jnp.float32)


def swap_kernel(
    n,
    slides,
    latents_in,
    keys_in,
    values_in,
    mask,
    count,
    weight,
    cot,
    pooled,
    grad_latents,
    grad_keys,
    grad_values,
    q_all,
    k_all,
    v_all,
    u_all,
    mask_own,
    mask_all,
    w_buf,
    cot_buf,
    u_own,
    probs,
    att,
    att_in,
    part_out,
    part_in,
    gk,
    gv,
    gq,
    gq_in,
    gq_sum,
    gl_in,
    latents,
    keys,
    values,
    local_sem,
    send_sem,
    recv_sem,
    slide_send,
    slide_recv,
    share_send,
    share_recv,
    head_send,
    head_recv,
):
    me = lax.axis_index("seq")
    my_head = lax.axis_index("head")
    my_slide = lax.axis_index("slide")
    rows = latents.shape[0]
    tiles = keys.shape[1]
    blk = k_all.shape[1]
    share = rows // slides
    heads = blk // HD
    width = latents.shape[1]
    all_rows = n * rows
    blocks = tiles // BLOCK
    factor = HD ** (-0.5)

    def cols(j):
        return pl.ds(pl.multiple_of(j * blk, 128), blk)

    def rows_of(j, size):
        return pl.ds(pl.multiple_of(j * size, 128), size)

    def peer(d):
        other, bit = me, 1
        while bit < n:
            if d & bit:
                other = other + bit - 2 * bit * lax.rem(lax.div(me, bit), 2)
            bit *= 2
        return other

    barrier = pltpu.get_barrier_semaphore()
    for d in range(1, n):
        pl.semaphore_signal(barrier, inc=1, device_id={"seq": peer(d)}, device_id_type=MESH)
    for e in range(1, slides):
        other = lax.rem(my_slide + e, slides)
        pl.semaphore_signal(barrier, inc=1, device_id={"slide": other}, device_id_type=MESH)
    pl.semaphore_signal(barrier, inc=1, device_id={"head": 1 - my_head}, device_id_type=MESH)

    def local(src, dst, i):
        copy = pltpu.make_async_copy(src, dst, local_sem.at[i])
        copy.start()
        return copy

    latents_copy = local(latents_in, latents, 12)
    keys_copy = local(keys_in, keys, 13)
    cot_copy = local(cot.at[0], cot_buf, 1)
    w_copy = local(weight, w_buf, 0)
    values_copy = local(values_in, values, 14)
    my_share = pl.ds(pl.multiple_of(my_slide * share, 16), share)
    mask_own[...] = jnp.zeros_like(mask_own)
    for b in range(blocks):
        mask_own[pl.ds(b, 1), :] = jnp.full((1, 128), mask[0, b], jnp.int32)
    mask_all[me] = mask_own[...]

    sent = []

    def send(kind, d, src, dst):
        copy = pltpu.make_async_remote_copy(
            src_ref=src,
            dst_ref=dst,
            send_sem=send_sem.at[kind, d - 1],
            recv_sem=recv_sem.at[kind, d - 1],
            device_id={"seq": peer(d)},
            device_id_type=MESH,
        )
        copy.start()
        sent.append(copy)
        return copy

    far = [n // 2] + [d for d in range(n - 1, 0, -1) if d != n // 2]
    pl.semaphore_wait(barrier, n - 1 + slides - 1 + 1)
    mask_moves = [send(0, d, mask_own, mask_all.at[me]) for d in far]
    latents_copy.wait()
    own_q = local(latents.at[my_share, cols(me)], q_all.at[me, my_slide], 2)
    q_moves = [send(1, d, latents.at[my_share, cols(peer(d))], q_all.at[me, my_slide]) for d in far]
    keys_copy.wait()
    own_k = local(keys.at[0, :, cols(me)], k_all.at[rows_of(me, tiles)], 3)
    k_moves = [send(2, d, keys.at[0, :, cols(peer(d))], k_all.at[rows_of(me, tiles)]) for d in far]

    live_count = count[0]
    w_copy.wait()
    cot_copy.wait()
    own_row = lax.broadcasted_iota(jnp.int32, (rows, 1), 0) + me * rows
    projected = dot(cot_buf[...], w_buf[...], ((1,), (1,)))
    u_own[...] = jnp.where(own_row < live_count, projected, 0.0).astype(jnp.bfloat16)
    own_u = local(u_own.at[:, cols(me)], u_all.at[rows_of(me, rows)], 5)
    u_moves = [send(4, d, u_own.at[:, cols(peer(d))], u_all.at[rows_of(me, rows)]) for d in far]

    values_copy.wait()
    own_v = local(values.at[0, :, cols(me)], v_all.at[rows_of(me, tiles)], 4)
    v_moves = [send(3, d, values.at[0, :, cols(peer(d))], v_all.at[rows_of(me, tiles)]) for d in far]

    lane = lax.broadcasted_iota(jnp.int32, (1, blk), 1) // HD

    def only(x, h):
        return jnp.where(lane == h, x, jnp.zeros_like(x))

    own_q.wait()
    for copy in q_moves:
        copy.wait_recv()
    share_moves = []
    for e in range(1, slides):
        copy = pltpu.make_async_remote_copy(
            src_ref=q_all.at[:, my_slide],
            dst_ref=q_all.at[:, my_slide],
            send_sem=share_send.at[e - 1],
            recv_sem=share_recv.at[e - 1],
            device_id={"slide": lax.rem(my_slide + e, slides)},
            device_id_type=MESH,
        )
        copy.start()
        share_moves.append(copy)
    own_k.wait()
    for copy in mask_moves + share_moves + k_moves:
        copy.wait_recv()
    q_rows = q_all[...].reshape(all_rows, blk)

    tops = []
    totals = []
    for h in range(heads):
        query = only(q_rows, h)

        def score_step(i, top, h=h, query=query):
            for b in range(blocks):
                at = pl.ds(pl.multiple_of(i * tiles + b * BLOCK, BLOCK), BLOCK)
                score = dot(k_all[at, :], query, ((1,), (1,))) * factor
                valid = jnp.broadcast_to(mask_all[i][b : b + 1, :1], (1, all_rows)) > 0
                score = jnp.where(valid, score, masked_score)
                probs[h, at, :] = score
                top = jnp.maximum(top, jnp.max(score, axis=0, keepdims=True))
            return top

        top = lax.fori_loop(0, n, score_step, jnp.full((1, all_rows), masked_score, jnp.float32))

        def exp_step(i, total, h=h, top=top):
            for b in range(blocks):
                at = pl.ds(pl.multiple_of(i * tiles + b * BLOCK, BLOCK), BLOCK)
                expos = jnp.exp(probs[h, at, :] - top)
                probs[h, at, :] = expos
                total = total + jnp.sum(expos, axis=0, keepdims=True)
            return total

        totals.append(lax.fori_loop(0, n, exp_step, jnp.zeros((1, all_rows), jnp.float32)))
    inverse = [1.0 / total for total in totals]

    own_u.wait()
    for copy in u_moves:
        copy.wait_recv()
    u_rows = u_all[...]
    gv_moves = []
    for d in far + [0]:
        j = peer(d)
        at = rows_of(j, tiles)
        grad_v = None
        for h in range(heads):
            weights = probs[h, at, :] * inverse[h]
            probs[h, at, :] = weights
            more_v = dot(weights.astype(jnp.bfloat16), only(u_rows, h), ((1,), (0,)))
            grad_v = more_v if grad_v is None else grad_v + more_v
        gv[at, :] = grad_v.astype(jnp.bfloat16)
        if d:
            gv_moves.append(send(7, d, gv.at[at], grad_values.at[0, :, cols(me)]))
        else:
            own_gv = local(gv.at[at], grad_values.at[0, :, cols(me)], 8)

    own_v.wait()
    for copy in v_moves:
        copy.wait_recv()

    def attend_step(i, sums):
        at = rows_of(i, tiles)
        v_block = v_all[at, :]
        for h in range(heads):
            weights = probs[h, at, :].astype(jnp.bfloat16)
            sums = sums + dot(only(v_block, h), weights, ((0,), (0,)))
        return sums

    zero = jnp.zeros((blk, all_rows), jnp.float32)
    attended = lax.fori_loop(0, n, attend_step, zero)
    every_row = lax.broadcasted_iota(jnp.int32, (1, all_rows), 1)
    attended = jnp.where(every_row < live_count, attended, 0.0)
    attended_rows = attended.T.astype(jnp.bfloat16)
    att[...] = attended_rows
    own_att = local(att.at[rows_of(me, rows)], att_in.at[:, cols(me)], 6)
    att_moves = [send(5, d, att.at[rows_of(peer(d), rows)], att_in.at[:, cols(me)]) for d in far]

    product = u_rows.astype(jnp.float32) * attended_rows.astype(jnp.float32)
    product = product.T
    delta = [jnp.sum(product[h * HD : (h + 1) * HD], axis=0, keepdims=True) for h in range(heads)]

    grad_q = zero
    gk_moves = []
    for d in far + [0]:
        j = peer(d)
        at = rows_of(j, tiles)
        v_block = v_all[at, :]
        k_block = k_all[at, :]
        grad_k = None
        for h in range(heads):
            query = only(q_rows, h)
            grad_prob = dot(v_block, only(u_rows, h), ((1,), (1,)))
            weights = probs[h, at, :]
            grad_score = (weights * (grad_prob - delta[h]) * factor).astype(jnp.bfloat16)
            more_k = dot(grad_score, query, ((1,), (0,)))
            grad_k = more_k if grad_k is None else grad_k + more_k
            grad_q = grad_q + dot(only(k_block, h), grad_score, ((0,), (0,)))
        gk[at, :] = grad_k.astype(jnp.bfloat16)
        if d:
            gk_moves.append(send(6, d, gk.at[at], grad_keys.at[0, :, cols(me)]))
        else:
            own_gk = local(gk.at[at], grad_keys.at[0, :, cols(me)], 7)

    grad_rows = grad_q.T
    gq[...] = grad_rows.astype(jnp.bfloat16)
    slide_moves = []
    for e in range(1, slides):
        copy = pltpu.make_async_remote_copy(
            src_ref=gq,
            dst_ref=gq_in.at[e - 1],
            send_sem=slide_send.at[e - 1],
            recv_sem=slide_recv.at[e - 1],
            device_id={"slide": lax.rem(my_slide + e, slides)},
            device_id_type=MESH,
        )
        copy.start()
        slide_moves.append(copy)

    own_att.wait()
    for copy in att_moves:
        copy.wait_recv()
    half = pooled.shape[2]
    mine = pl.ds(pl.multiple_of(my_head * half, 128), half)
    theirs = pl.ds(pl.multiple_of((1 - my_head) * half, 128), half)
    part_out[...] = dot(att_in[...], w_buf[:, theirs], ((1,), (0,))).astype(jnp.bfloat16)
    head_move = pltpu.make_async_remote_copy(
        src_ref=part_out,
        dst_ref=part_in,
        send_sem=head_send,
        recv_sem=head_recv,
        device_id={"head": 1 - my_head},
        device_id_type=MESH,
    )
    head_move.start()
    own_part = dot(att_in[...], w_buf[:, mine], ((1,), (0,)))

    total = grad_rows
    for e, copy in enumerate(slide_moves):
        copy.wait_recv()
        total = total + gq_in[e].astype(jnp.float32)
    gq_sum[...] = total.astype(jnp.bfloat16)
    own_gl = local(gq_sum.at[rows_of(me, rows)], gl_in.at[:, cols(me)], 9)
    gl_moves = [send(8, d, gq_sum.at[rows_of(peer(d), rows)], gl_in.at[:, cols(me)]) for d in far]

    head_move.wait_recv()
    pooled[0] = (own_part + part_in[...].astype(jnp.float32)).astype(jnp.bfloat16)

    own_gl.wait()
    for copy in gl_moves:
        copy.wait_recv()
    grad_latents[...] = gl_in[...].astype(jnp.float32)
    own_gk.wait()
    own_gv.wait()
    for copy in gk_moves + gv_moves:
        copy.wait_recv()
    for copy in sent + slide_moves + share_moves + [head_move]:
        copy.wait_send()


def finish_kernel(count, *refs):
    sems = refs[-1]
    copies = [pltpu.make_async_copy(refs[i], refs[count + i], sems.at[i]) for i in range(count)]
    for copy in copies:
        copy.start()
    for copy in copies:
        copy.wait()


def swapped_body(latents, tile_keys, tile_values, tile_mask, latent_counts, out_weight, cotangent):
    n = lax.axis_size("seq")
    slides = lax.axis_size("slide")
    rows, width = latents.shape
    tiles = tile_keys.shape[1]
    depth = out_weight.shape[1]
    blk = width // n
    heads = blk // HD
    half = depth // 2
    bf16 = jnp.bfloat16
    anywhere = pl.BlockSpec(memory_space=pl.ANY)
    scalars = pl.BlockSpec(memory_space=pltpu.SMEM)
    dma = pltpu.SemaphoreType.DMA
    flops = 2 * heads * 6 * n * rows * n * tiles * HD + 4 * rows * width * depth
    results = pl.pallas_call(
        functools.partial(swap_kernel, n, slides),
        out_shape=(
            pltpu.VMEM((1, rows, half), bf16),
            pltpu.VMEM((rows, width), jnp.float32),
            pltpu.VMEM(tile_keys.shape, bf16),
            pltpu.VMEM(tile_values.shape, bf16),
        ),
        in_specs=[anywhere, anywhere, anywhere, scalars, scalars, anywhere, anywhere],
        out_specs=(pl.BlockSpec(memory_space=pltpu.VMEM),) * 4,
        scratch_shapes=[
            pltpu.VMEM((n, slides, rows // slides, blk), bf16),
            pltpu.VMEM((n * tiles, blk), bf16),
            pltpu.VMEM((n * tiles, blk), bf16),
            pltpu.VMEM((n * rows, blk), bf16),
            pltpu.VMEM((8 * pl.cdiv(tiles // BLOCK, 8), 128), jnp.int32),
            pltpu.VMEM((n, 8 * pl.cdiv(tiles // BLOCK, 8), 128), jnp.int32),
            pltpu.VMEM((width, depth), bf16),
            pltpu.VMEM((rows, depth), bf16),
            pltpu.VMEM((rows, width), bf16),
            pltpu.VMEM((heads, n * tiles, n * rows), jnp.float32),
            pltpu.VMEM((n * rows, blk), bf16),
            pltpu.VMEM((rows, width), bf16),
            pltpu.VMEM((rows, half), bf16),
            pltpu.VMEM((rows, half), bf16),
            pltpu.VMEM((n * tiles, blk), bf16),
            pltpu.VMEM((n * tiles, blk), bf16),
            pltpu.VMEM((n * rows, blk), bf16),
            pltpu.VMEM((slides - 1, n * rows, blk), bf16),
            pltpu.VMEM((n * rows, blk), bf16),
            pltpu.VMEM((rows, width), bf16),
            pltpu.VMEM(latents.shape, bf16),
            pltpu.VMEM(tile_keys.shape, bf16),
            pltpu.VMEM(tile_values.shape, bf16),
            dma((15,)),
            dma((9, n - 1)),
            dma((9, n - 1)),
            dma((slides - 1,)),
            dma((slides - 1,)),
            dma((slides - 1,)),
            dma((slides - 1,)),
            dma,
            dma,
        ],
        compiler_params=pltpu.CompilerParams(
            collective_id=0, has_side_effects=True, vmem_limit_bytes=60 * 1024 * 1024
        ),
        cost_estimate=pl.CostEstimate(
            flops=flops, bytes_accessed=8 * rows * depth * 2, transcendentals=heads * n * rows * n * tiles
        ),
    )(latents, tile_keys, tile_values, tile_mask, latent_counts, out_weight, cotangent)
    return pl.pallas_call(
        functools.partial(finish_kernel, len(results)),
        out_shape=tuple(jax.ShapeDtypeStruct(x.shape, x.dtype) for x in results),
        in_specs=[anywhere] * len(results),
        out_specs=(anywhere,) * len(results),
        scratch_shapes=[dma((len(results),))],
        compiler_params=pltpu.CompilerParams(vmem_limit_bytes=4 * 1024 * 1024),
    )(*results)


def body(latents, tile_keys, tile_values, tile_mask, latent_counts, out_weight, cotangent):
    local_rows = latents.shape[0]
    local_width = latents.shape[1]
    head_count = local_width // HD
    factor = HD ** (-0.5)
    queries = lax.all_gather(latents, "seq", axis=0, tiled=True)
    total_rows = queries.shape[0]
    first_row = lax.axis_index("seq") * local_rows
    every_row = lax.broadcasted_iota(jnp.int32, (total_rows, 1), 0)
    own_row = lax.broadcasted_iota(jnp.int32, (local_rows, 1), 0) + first_row
    tile_count = tile_keys.shape[1]
    key_block = tile_keys[0]
    value_block = tile_values[0]
    valid_tiles = jnp.broadcast_to(tile_mask[0][:, None] > 0, (tile_count // BLOCK, BLOCK)).reshape(
        1, tile_count
    )
    live_count = latent_counts[0]
    score_list = []
    for which_head in range(head_count):
        columns = slice(which_head * HD, (which_head + 1) * HD)
        raw_scores = (
            jnp.einsum(
                "qc,tc->qt",
                queries[:, columns],
                key_block[:, columns],
                preferred_element_type=jnp.float32,
            )
            * factor
        )
        score_list.append(jnp.where(valid_tiles, raw_scores, masked_score))
    local_top = jnp.stack([jnp.max(scored, axis=1) for scored in score_list], axis=1)
    row_top = lax.pmax(local_top, "seq")
    expo_list = []
    weighted_list = []
    total_list = []
    for which_head in range(head_count):
        columns = slice(which_head * HD, (which_head + 1) * HD)
        expos = jnp.where(
            valid_tiles,
            jnp.exp(score_list[which_head] - row_top[:, which_head : which_head + 1]),
            0.0,
        )
        expo_list.append(expos)
        total_list.append(jnp.sum(expos, axis=1))
        weighted_list.append(
            jnp.dot(
                expos.astype(jnp.bfloat16),
                value_block[:, columns],
                preferred_element_type=jnp.float32,
            )
        )
    partial_sums = jnp.concatenate(weighted_list, axis=1)
    partial_totals = jnp.stack(total_list, axis=1)
    weighted, totals = lax.psum((partial_sums, partial_totals), "seq")
    span = weighted.shape[0]
    attended = jnp.where(
        every_row < live_count,
        (weighted.reshape(span, head_count, HD) / totals[:, :, None]).reshape(span, local_width),
        0.0,
    ).astype(jnp.bfloat16)
    own_attended = lax.dynamic_slice_in_dim(attended, first_row, local_rows, 0)
    pooled_part = jnp.dot(own_attended, out_weight, preferred_element_type=jnp.float32)
    pooled_parts = [
        lax.psum_scatter(pooled_part.astype(jnp.bfloat16), "head", scatter_dimension=1, tiled=True)
    ]
    projected = jnp.einsum(
        "rd,cd->rc", cotangent[0], out_weight, preferred_element_type=jnp.float32
    )
    upstream = jnp.where(own_row < live_count, projected, 0.0).astype(jnp.bfloat16)
    upstream_all = lax.all_gather(upstream, "seq", axis=0, tiled=True)
    row_delta = jnp.sum(
        (upstream_all.astype(jnp.float32) * attended.astype(jnp.float32)).reshape(
            total_rows, head_count, HD
        ),
        axis=2,
    )
    query_list = []
    key_list = []
    value_list = []
    for which_head in range(head_count):
        columns = slice(which_head * HD, (which_head + 1) * HD)
        up_head = upstream_all[:, columns]
        weights = expo_list[which_head] / totals[:, which_head : which_head + 1]
        value_list.append(
            jnp.einsum(
                "qt,qc->tc",
                weights.astype(jnp.bfloat16),
                up_head,
                preferred_element_type=jnp.float32,
            )
        )
        grad_prob = jnp.einsum(
            "qc,tc->qt", up_head, value_block[:, columns], preferred_element_type=jnp.float32
        )
        grad_score = (
            weights * (grad_prob - row_delta[:, which_head : which_head + 1]) * factor
        ).astype(jnp.bfloat16)
        query_list.append(
            jnp.dot(grad_score, key_block[:, columns], preferred_element_type=jnp.float32)
        )
        key_list.append(
            jnp.einsum(
                "qt,qc->tc", grad_score, queries[:, columns], preferred_element_type=jnp.float32
            )
        )
    grad_rows = jnp.concatenate(query_list, axis=1)
    key_grads = [jnp.concatenate(key_list, axis=1).astype(jnp.bfloat16)]
    value_grads = [jnp.concatenate(value_list, axis=1).astype(jnp.bfloat16)]
    own_grad = lax.psum_scatter(
        grad_rows.astype(jnp.bfloat16), "seq", scatter_dimension=0, tiled=True
    )
    grad_latents = lax.psum(own_grad, "slide").astype(jnp.float32)
    return (
        jnp.stack(pooled_parts, axis=0),
        grad_latents,
        jnp.stack(key_grads, axis=0),
        jnp.stack(value_grads, axis=0),
    )


def solution(mesh):
    placed = (
        P(("groups", "seq"), "head"),
        P(("groups", "slide"), "seq", "head"),
        P(("groups", "slide"), "seq", "head"),
        P(("groups", "slide"), "seq"),
        P(("groups", "slide")),
        P("head", None),
        P(("groups", "slide"), "seq", None),
    )
    block_width = 128 * mesh.shape["seq"]
    swapped = mesh.shape["seq"] in (2, 4, 8) and mesh.shape["slide"] > 1 and mesh.shape["head"] == 2

    def chosen(latents, *others):
        by_heads = swapped and latents.shape[1] % block_width == 0
        by_heads = by_heads and latents.shape[0] % 128 == 0
        by_heads = by_heads and latents.shape[0] % (16 * mesh.shape["slide"]) == 0 and others[0].shape[1] % BLOCK == 0
        return (swapped_body if by_heads else body)(latents, *others)

    return jax.shard_map(
        chosen,
        mesh=mesh,
        in_specs=placed,
        out_specs=(
            P(("groups", "slide"), "seq", "head"),
            P(("groups", "seq"), "head"),
            P(("groups", "slide"), "seq", "head"),
            P(("groups", "slide"), "seq", "head"),
        ),
        check_vma=False,
    )
```

```python
import functools

import jax
import jax.numpy as jnp
from jax import lax
from jax.experimental import pallas as pl
from jax.experimental.pallas import tpu as pltpu
from jax.sharding import PartitionSpec as P

HD = 64
BLOCK = 128


masked_score = -1e30


MESH = pl.DeviceIdType.MESH


def dot(a, b, dims):
    return lax.dot_general(a, b, (dims, ((), ())), preferred_element_type=jnp.float32)


def swap_kernel(
    n,
    slides,
    latents_in,
    keys_in,
    values_in,
    mask,
    count,
    weight,
    cot,
    pooled,
    grad_latents,
    grad_keys,
    grad_values,
    q_all,
    k_all,
    v_all,
    u_all,
    mask_own,
    mask_all,
    w_buf,
    cot_buf,
    u_own,
    probs,
    att,
    att_in,
    part_out,
    part_in,
    gk,
    gv,
    gq,
    gq_in,
    gq_sum,
    gl_in,
    latents,
    keys,
    values,
    local_sem,
    send_sem,
    recv_sem,
    slide_send,
    slide_recv,
    share_send,
    share_recv,
    head_send,
    head_recv,
):
    me = lax.axis_index("seq")
    my_head = lax.axis_index("head")
    my_slide = lax.axis_index("slide")
    rows = latents.shape[0]
    tiles = keys.shape[1]
    blk = k_all.shape[1]
    share = rows // slides
    heads = blk // HD
    width = latents.shape[1]
    all_rows = n * rows
    blocks = tiles // BLOCK
    factor = HD ** (-0.5)

    def cols(j):
        return pl.ds(pl.multiple_of(j * blk, 128), blk)

    def rows_of(j, size):
        return pl.ds(pl.multiple_of(j * size, 128), size)

    def peer(d):
        other, bit = me, 1
        while bit < n:
            if d & bit:
                other = other + bit - 2 * bit * lax.rem(lax.div(me, bit), 2)
            bit *= 2
        return other

    barrier = pltpu.get_barrier_semaphore()
    for d in range(1, n):
        pl.semaphore_signal(barrier, inc=1, device_id={"seq": peer(d)}, device_id_type=MESH)
    for e in range(1, slides):
        other = lax.rem(my_slide + e, slides)
        pl.semaphore_signal(barrier, inc=1, device_id={"slide": other}, device_id_type=MESH)
    pl.semaphore_signal(barrier, inc=1, device_id={"head": 1 - my_head}, device_id_type=MESH)

    def local(src, dst, i):
        copy = pltpu.make_async_copy(src, dst, local_sem.at[i])
        copy.start()
        return copy

    latents_copy = local(latents_in, latents, 12)
    keys_copy = local(keys_in, keys, 13)
    cot_copy = local(cot.at[0], cot_buf, 1)
    w_copy = local(weight, w_buf, 0)
    values_copy = local(values_in, values, 14)
    my_share = pl.ds(pl.multiple_of(my_slide * share, 16), share)
    mask_own[...] = jnp.zeros_like(mask_own)
    for b in range(blocks):
        mask_own[pl.ds(b, 1), :] = jnp.full((1, 128), mask[0, b], jnp.int32)
    mask_all[me] = mask_own[...]

    sent = []

    def send(kind, d, src, dst):
        copy = pltpu.make_async_remote_copy(
            src_ref=src,
            dst_ref=dst,
            send_sem=send_sem.at[kind, d - 1],
            recv_sem=recv_sem.at[kind, d - 1],
            device_id={"seq": peer(d)},
            device_id_type=MESH,
        )
        copy.start()
        sent.append(copy)
        return copy

    far = [n // 2] + [d for d in range(n - 1, 0, -1) if d != n // 2]
    pl.semaphore_wait(barrier, n - 1 + slides - 1 + 1)
    mask_moves = [send(0, d, mask_own, mask_all.at[me]) for d in far]
    latents_copy.wait()
    own_q = local(latents.at[my_share, cols(me)], q_all.at[me, my_slide], 2)
    q_moves = [send(1, d, latents.at[my_share, cols(peer(d))], q_all.at[me, my_slide]) for d in far]
    keys_copy.wait()
    own_k = local(keys.at[0, :, cols(me)], k_all.at[rows_of(me, tiles)], 3)
    k_moves = [send(2, d, keys.at[0, :, cols(peer(d))], k_all.at[rows_of(me, tiles)]) for d in far]

    live_count = count[0]
    w_copy.wait()
    cot_copy.wait()
    own_row = lax.broadcasted_iota(jnp.int32, (rows, 1), 0) + me * rows
    projected = dot(cot_buf[...], w_buf[...], ((1,), (1,)))
    u_own[...] = jnp.where(own_row < live_count, projected, 0.0).astype(jnp.bfloat16)
    own_u = local(u_own.at[:, cols(me)], u_all.at[rows_of(me, rows)], 5)
    u_moves = [send(4, d, u_own.at[:, cols(peer(d))], u_all.at[rows_of(me, rows)]) for d in far]

    lane = lax.broadcasted_iota(jnp.int32, (1, blk), 1) // HD

    def only(x, h):
        return jnp.where(lane == h, x, jnp.zeros_like(x))

    own_q.wait()
    for copy in q_moves:
        copy.wait_recv()
    share_moves = []
    for e in range(1, slides):
        copy = pltpu.make_async_remote_copy(
            src_ref=q_all.at[:, my_slide],
            dst_ref=q_all.at[:, my_slide],
            send_sem=share_send.at[e - 1],
            recv_sem=share_recv.at[e - 1],
            device_id={"slide": lax.rem(my_slide + e, slides)},
            device_id_type=MESH,
        )
        copy.start()
        share_moves.append(copy)
    own_k.wait()
    for copy in mask_moves + share_moves + k_moves:
        copy.wait_recv()
    values_copy.wait()
    own_v = local(values.at[0, :, cols(me)], v_all.at[rows_of(me, tiles)], 4)
    v_moves = [send(3, d, values.at[0, :, cols(peer(d))], v_all.at[rows_of(me, tiles)]) for d in far]

    q_rows = q_all[...].reshape(all_rows, blk)

    tops = []
    totals = []
    for h in range(heads):
        query = only(q_rows, h)

        def score_step(i, top, h=h, query=query):
            scores = dot(k_all[rows_of(i, tiles), :], query, ((1,), (1,))) * factor
            for b in range(blocks):
                at = pl.ds(pl.multiple_of(i * tiles + b * BLOCK, BLOCK), BLOCK)
                score = scores[b * BLOCK : (b + 1) * BLOCK]
                valid = jnp.broadcast_to(mask_all[i][b : b + 1, :1], (1, all_rows)) > 0
                score = jnp.where(valid, score, masked_score)
                probs[h, at, :] = score
                top = jnp.maximum(top, jnp.max(score, axis=0, keepdims=True))
            return top

        top = lax.fori_loop(0, n, score_step, jnp.full((1, all_rows), masked_score, jnp.float32))

        def exp_step(i, total, h=h, top=top):
            for b in range(blocks):
                at = pl.ds(pl.multiple_of(i * tiles + b * BLOCK, BLOCK), BLOCK)
                expos = jnp.exp(probs[h, at, :] - top)
                probs[h, at, :] = expos
                total = total + jnp.sum(expos, axis=0, keepdims=True)
            return total

        totals.append(lax.fori_loop(0, n, exp_step, jnp.zeros((1, all_rows), jnp.float32)))
    inverse = [1.0 / total for total in totals]

    own_u.wait()
    for copy in u_moves:
        copy.wait_recv()
    u_rows = u_all[...]
    gv_moves = []
    for d in far + [0]:
        j = peer(d)
        at = rows_of(j, tiles)
        grad_v = None
        for h in range(heads):
            weights = probs[h, at, :] * inverse[h]
            probs[h, at, :] = weights
            more_v = dot(weights.astype(jnp.bfloat16), only(u_rows, h), ((1,), (0,)))
            grad_v = more_v if grad_v is None else grad_v + more_v
        gv[at, :] = grad_v.astype(jnp.bfloat16)
        if d:
            gv_moves.append(send(7, d, gv.at[at], grad_values.at[0, :, cols(me)]))
        else:
            own_gv = local(gv.at[at], grad_values.at[0, :, cols(me)], 8)

    own_v.wait()
    for copy in v_moves:
        copy.wait_recv()

    def attend_step(i, sums):
        at = rows_of(i, tiles)
        v_block = v_all[at, :]
        for h in range(heads):
            weights = probs[h, at, :].astype(jnp.bfloat16)
            sums = sums + dot(only(v_block, h), weights, ((0,), (0,)))
        return sums

    zero = jnp.zeros((blk, all_rows), jnp.float32)
    attended = lax.fori_loop(0, n, attend_step, zero)
    every_row = lax.broadcasted_iota(jnp.int32, (1, all_rows), 1)
    attended = jnp.where(every_row < live_count, attended, 0.0)
    attended_rows = attended.T.astype(jnp.bfloat16)
    att[...] = attended_rows
    own_att = local(att.at[rows_of(me, rows)], att_in.at[:, cols(me)], 6)
    att_moves = [send(5, d, att.at[rows_of(peer(d), rows)], att_in.at[:, cols(me)]) for d in far]

    product = u_rows.astype(jnp.float32) * attended_rows.astype(jnp.float32)
    product = product.T
    delta = [jnp.sum(product[h * HD : (h + 1) * HD], axis=0, keepdims=True) for h in range(heads)]

    grad_q = zero
    gk_moves = []
    for d in far + [0]:
        j = peer(d)
        at = rows_of(j, tiles)
        v_block = v_all[at, :]
        k_block = k_all[at, :]
        grad_k = None
        for h in range(heads):
            query = only(q_rows, h)
            grad_prob = dot(v_block, only(u_rows, h), ((1,), (1,)))
            weights = probs[h, at, :]
            grad_score = (weights * (grad_prob - delta[h]) * factor).astype(jnp.bfloat16)
            more_k = dot(grad_score, query, ((1,), (0,)))
            grad_k = more_k if grad_k is None else grad_k + more_k
            grad_q = grad_q + dot(only(k_block, h), grad_score, ((0,), (0,)))
        gk[at, :] = grad_k.astype(jnp.bfloat16)
        if d:
            gk_moves.append(send(6, d, gk.at[at], grad_keys.at[0, :, cols(me)]))
        else:
            own_gk = local(gk.at[at], grad_keys.at[0, :, cols(me)], 7)

    grad_rows = grad_q.T
    gq[...] = grad_rows.astype(jnp.bfloat16)
    slide_moves = []
    for e in range(1, slides):
        copy = pltpu.make_async_remote_copy(
            src_ref=gq,
            dst_ref=gq_in.at[e - 1],
            send_sem=slide_send.at[e - 1],
            recv_sem=slide_recv.at[e - 1],
            device_id={"slide": lax.rem(my_slide + e, slides)},
            device_id_type=MESH,
        )
        copy.start()
        slide_moves.append(copy)

    own_att.wait()
    for copy in att_moves:
        copy.wait_recv()
    half = pooled.shape[2]
    mine = pl.ds(pl.multiple_of(my_head * half, 128), half)
    theirs = pl.ds(pl.multiple_of((1 - my_head) * half, 128), half)
    part_out[...] = dot(att_in[...], w_buf[:, theirs], ((1,), (0,))).astype(jnp.bfloat16)
    head_move = pltpu.make_async_remote_copy(
        src_ref=part_out,
        dst_ref=part_in,
        send_sem=head_send,
        recv_sem=head_recv,
        device_id={"head": 1 - my_head},
        device_id_type=MESH,
    )
    head_move.start()
    own_part = dot(att_in[...], w_buf[:, mine], ((1,), (0,)))

    total = grad_rows
    for e, copy in enumerate(slide_moves):
        copy.wait_recv()
        total = total + gq_in[e].astype(jnp.float32)
    gq_sum[...] = total.astype(jnp.bfloat16)
    own_gl = local(gq_sum.at[rows_of(me, rows)], gl_in.at[:, cols(me)], 9)
    gl_moves = [send(8, d, gq_sum.at[rows_of(peer(d), rows)], gl_in.at[:, cols(me)]) for d in far]

    head_move.wait_recv()
    pooled[0] = (own_part + part_in[...].astype(jnp.float32)).astype(jnp.bfloat16)

    own_gl.wait()
    for copy in gl_moves:
        copy.wait_recv()
    grad_latents[...] = gl_in[...].astype(jnp.float32)
    own_gk.wait()
    own_gv.wait()
    for copy in gk_moves + gv_moves:
        copy.wait_recv()
    for copy in sent + slide_moves + share_moves + [head_move]:
        copy.wait_send()


def finish_kernel(count, *refs):
    sems = refs[-1]
    copies = [pltpu.make_async_copy(refs[i], refs[count + i], sems.at[i]) for i in range(count)]
    for copy in copies:
        copy.start()
    for copy in copies:
        copy.wait()


def swapped_body(latents, tile_keys, tile_values, tile_mask, latent_counts, out_weight, cotangent):
    n = lax.axis_size("seq")
    slides = lax.axis_size("slide")
    rows, width = latents.shape
    tiles = tile_keys.shape[1]
    depth = out_weight.shape[1]
    blk = width // n
    heads = blk // HD
    half = depth // 2
    bf16 = jnp.bfloat16
    anywhere = pl.BlockSpec(memory_space=pl.ANY)
    scalars = pl.BlockSpec(memory_space=pltpu.SMEM)
    dma = pltpu.SemaphoreType.DMA
    flops = 2 * heads * 6 * n * rows * n * tiles * HD + 4 * rows * width * depth
    results = pl.pallas_call(
        functools.partial(swap_kernel, n, slides),
        out_shape=(
            pltpu.VMEM((1, rows, half), bf16),
            pltpu.VMEM((rows, width), jnp.float32),
            pltpu.VMEM(tile_keys.shape, bf16),
            pltpu.VMEM(tile_values.shape, bf16),
        ),
        in_specs=[anywhere, anywhere, anywhere, scalars, scalars, anywhere, anywhere],
        out_specs=(pl.BlockSpec(memory_space=pltpu.VMEM),) * 4,
        scratch_shapes=[
            pltpu.VMEM((n, slides, rows // slides, blk), bf16),
            pltpu.VMEM((n * tiles, blk), bf16),
            pltpu.VMEM((n * tiles, blk), bf16),
            pltpu.VMEM((n * rows, blk), bf16),
            pltpu.VMEM((8 * pl.cdiv(tiles // BLOCK, 8), 128), jnp.int32),
            pltpu.VMEM((n, 8 * pl.cdiv(tiles // BLOCK, 8), 128), jnp.int32),
            pltpu.VMEM((width, depth), bf16),
            pltpu.VMEM((rows, depth), bf16),
            pltpu.VMEM((rows, width), bf16),
            pltpu.VMEM((heads, n * tiles, n * rows), jnp.float32),
            pltpu.VMEM((n * rows, blk), bf16),
            pltpu.VMEM((rows, width), bf16),
            pltpu.VMEM((rows, half), bf16),
            pltpu.VMEM((rows, half), bf16),
            pltpu.VMEM((n * tiles, blk), bf16),
            pltpu.VMEM((n * tiles, blk), bf16),
            pltpu.VMEM((n * rows, blk), bf16),
            pltpu.VMEM((slides - 1, n * rows, blk), bf16),
            pltpu.VMEM((n * rows, blk), bf16),
            pltpu.VMEM((rows, width), bf16),
            pltpu.VMEM(latents.shape, bf16),
            pltpu.VMEM(tile_keys.shape, bf16),
            pltpu.VMEM(tile_values.shape, bf16),
            dma((15,)),
            dma((9, n - 1)),
            dma((9, n - 1)),
            dma((slides - 1,)),
            dma((slides - 1,)),
            dma((slides - 1,)),
            dma((slides - 1,)),
            dma,
            dma,
        ],
        compiler_params=pltpu.CompilerParams(
            collective_id=0, has_side_effects=True, vmem_limit_bytes=60 * 1024 * 1024
        ),
        cost_estimate=pl.CostEstimate(
            flops=flops, bytes_accessed=8 * rows * depth * 2, transcendentals=heads * n * rows * n * tiles
        ),
    )(latents, tile_keys, tile_values, tile_mask, latent_counts, out_weight, cotangent)
    return pl.pallas_call(
        functools.partial(finish_kernel, len(results)),
        out_shape=tuple(jax.ShapeDtypeStruct(x.shape, x.dtype) for x in results),
        in_specs=[anywhere] * len(results),
        out_specs=(anywhere,) * len(results),
        scratch_shapes=[dma((len(results),))],
        compiler_params=pltpu.CompilerParams(vmem_limit_bytes=4 * 1024 * 1024),
    )(*results)


def body(latents, tile_keys, tile_values, tile_mask, latent_counts, out_weight, cotangent):
    local_rows = latents.shape[0]
    local_width = latents.shape[1]
    head_count = local_width // HD
    factor = HD ** (-0.5)
    queries = lax.all_gather(latents, "seq", axis=0, tiled=True)
    total_rows = queries.shape[0]
    first_row = lax.axis_index("seq") * local_rows
    every_row = lax.broadcasted_iota(jnp.int32, (total_rows, 1), 0)
    own_row = lax.broadcasted_iota(jnp.int32, (local_rows, 1), 0) + first_row
    tile_count = tile_keys.shape[1]
    key_block = tile_keys[0]
    value_block = tile_values[0]
    valid_tiles = jnp.broadcast_to(tile_mask[0][:, None] > 0, (tile_count // BLOCK, BLOCK)).reshape(
        1, tile_count
    )
    live_count = latent_counts[0]
    score_list = []
    for which_head in range(head_count):
        columns = slice(which_head * HD, (which_head + 1) * HD)
        raw_scores = (
            jnp.einsum(
                "qc,tc->qt",
                queries[:, columns],
                key_block[:, columns],
                preferred_element_type=jnp.float32,
            )
            * factor
        )
        score_list.append(jnp.where(valid_tiles, raw_scores, masked_score))
    local_top = jnp.stack([jnp.max(scored, axis=1) for scored in score_list], axis=1)
    row_top = lax.pmax(local_top, "seq")
    expo_list = []
    weighted_list = []
    total_list = []
    for which_head in range(head_count):
        columns = slice(which_head * HD, (which_head + 1) * HD)
        expos = jnp.where(
            valid_tiles,
            jnp.exp(score_list[which_head] - row_top[:, which_head : which_head + 1]),
            0.0,
        )
        expo_list.append(expos)
        total_list.append(jnp.sum(expos, axis=1))
        weighted_list.append(
            jnp.dot(
                expos.astype(jnp.bfloat16),
                value_block[:, columns],
                preferred_element_type=jnp.float32,
            )
        )
    partial_sums = jnp.concatenate(weighted_list, axis=1)
    partial_totals = jnp.stack(total_list, axis=1)
    weighted, totals = lax.psum((partial_sums, partial_totals), "seq")
    span = weighted.shape[0]
    attended = jnp.where(
        every_row < live_count,
        (weighted.reshape(span, head_count, HD) / totals[:, :, None]).reshape(span, local_width),
        0.0,
    ).astype(jnp.bfloat16)
    own_attended = lax.dynamic_slice_in_dim(attended, first_row, local_rows, 0)
    pooled_part = jnp.dot(own_attended, out_weight, preferred_element_type=jnp.float32)
    pooled_parts = [
        lax.psum_scatter(pooled_part.astype(jnp.bfloat16), "head", scatter_dimension=1, tiled=True)
    ]
    projected = jnp.einsum(
        "rd,cd->rc", cotangent[0], out_weight, preferred_element_type=jnp.float32
    )
    upstream = jnp.where(own_row < live_count, projected, 0.0).astype(jnp.bfloat16)
    upstream_all = lax.all_gather(upstream, "seq", axis=0, tiled=True)
    row_delta = jnp.sum(
        (upstream_all.astype(jnp.float32) * attended.astype(jnp.float32)).reshape(
            total_rows, head_count, HD
        ),
        axis=2,
    )
    query_list = []
    key_list = []
    value_list = []
    for which_head in range(head_count):
        columns = slice(which_head * HD, (which_head + 1) * HD)
        up_head = upstream_all[:, columns]
        weights = expo_list[which_head] / totals[:, which_head : which_head + 1]
        value_list.append(
            jnp.einsum(
                "qt,qc->tc",
                weights.astype(jnp.bfloat16),
                up_head,
                preferred_element_type=jnp.float32,
            )
        )
        grad_prob = jnp.einsum(
            "qc,tc->qt", up_head, value_block[:, columns], preferred_element_type=jnp.float32
        )
        grad_score = (
            weights * (grad_prob - row_delta[:, which_head : which_head + 1]) * factor
        ).astype(jnp.bfloat16)
        query_list.append(
            jnp.dot(grad_score, key_block[:, columns], preferred_element_type=jnp.float32)
        )
        key_list.append(
            jnp.einsum(
                "qt,qc->tc", grad_score, queries[:, columns], preferred_element_type=jnp.float32
            )
        )
    grad_rows = jnp.concatenate(query_list, axis=1)
    key_grads = [jnp.concatenate(key_list, axis=1).astype(jnp.bfloat16)]
    value_grads = [jnp.concatenate(value_list, axis=1).astype(jnp.bfloat16)]
    own_grad = lax.psum_scatter(
        grad_rows.astype(jnp.bfloat16), "seq", scatter_dimension=0, tiled=True
    )
    grad_latents = lax.psum(own_grad, "slide").astype(jnp.float32)
    return (
        jnp.stack(pooled_parts, axis=0),
        grad_latents,
        jnp.stack(key_grads, axis=0),
        jnp.stack(value_grads, axis=0),
    )


def solution(mesh):
    placed = (
        P(("groups", "seq"), "head"),
        P(("groups", "slide"), "seq", "head"),
        P(("groups", "slide"), "seq", "head"),
        P(("groups", "slide"), "seq"),
        P(("groups", "slide")),
        P("head", None),
        P(("groups", "slide"), "seq", None),
    )
    block_width = 128 * mesh.shape["seq"]
    swapped = mesh.shape["seq"] in (2, 4, 8) and mesh.shape["slide"] > 1 and mesh.shape["head"] == 2

    def chosen(latents, *others):
        by_heads = swapped and latents.shape[1] % block_width == 0
        by_heads = by_heads and latents.shape[0] % 128 == 0
        by_heads = by_heads and latents.shape[0] % (16 * mesh.shape["slide"]) == 0 and others[0].shape[1] % BLOCK == 0
        return (swapped_body if by_heads else body)(latents, *others)

    return jax.shard_map(
        chosen,
        mesh=mesh,
        in_specs=placed,
        out_specs=(
            P(("groups", "slide"), "seq", "head"),
            P(("groups", "seq"), "head"),
            P(("groups", "slide"), "seq", "head"),
            P(("groups", "slide"), "seq", "head"),
        ),
        check_vma=False,
    )
```

```python
import functools

import jax
import jax.numpy as jnp
from jax import lax
from jax.experimental import pallas as pl
from jax.experimental.pallas import tpu as pltpu
from jax.sharding import PartitionSpec as P

HD = 64
BLOCK = 128


masked_score = -1e30


MESH = pl.DeviceIdType.MESH
PAIR = 2


def dot(a, b, dims):
    return lax.dot_general(a, b, (dims, ((), ())), preferred_element_type=jnp.float32)


def swap_kernel(
    n,
    slides,
    latents_in,
    keys_in,
    values_in,
    mask,
    count,
    weight,
    cot,
    pooled,
    grad_latents,
    grad_keys,
    grad_values,
    q_all,
    k_all,
    v_all,
    u_all,
    mask_own,
    mask_all,
    w_buf,
    cot_buf,
    u_own,
    probs,
    att,
    att_in,
    part_out,
    part_in,
    gk,
    gv,
    gq,
    gq_in,
    gq_sum,
    gl_in,
    latents,
    keys,
    values,
    stats,
    stats_in,
    deltas,
    deltas_in,
    local_sem,
    send_sem,
    recv_sem,
    slide_send,
    slide_recv,
    share_send,
    share_recv,
    head_send,
    head_recv,
):
    me = lax.axis_index("seq")
    g = PAIR
    side = lax.rem(me, g)
    part = lax.div(me, g)
    my_head = lax.axis_index("head")
    my_slide = lax.axis_index("slide")
    rows = latents.shape[0]
    tiles = keys.shape[1]
    blk = k_all.shape[1]
    share = rows // slides
    heads = blk // HD
    width = latents.shape[1]
    all_rows = n * rows
    blocks = tiles // BLOCK
    factor = HD ** (-0.5)

    def cols(j):
        return pl.ds(pl.multiple_of(j * blk, 128), blk)

    def rows_of(j, size):
        return pl.ds(pl.multiple_of(j * size, 128), size)

    def cols_for(d):
        return cols(lax.rem(peer(d), g))

    def peer(d):
        other, bit = me, 1
        while bit < n:
            if d & bit:
                other = other + bit - 2 * bit * lax.rem(lax.div(me, bit), 2)
            bit *= 2
        return other

    barrier = pltpu.get_barrier_semaphore()
    for d in range(1, n):
        pl.semaphore_signal(barrier, inc=1, device_id={"seq": peer(d)}, device_id_type=MESH)
    for e in range(1, slides):
        other = lax.rem(my_slide + e, slides)
        pl.semaphore_signal(barrier, inc=1, device_id={"slide": other}, device_id_type=MESH)
    pl.semaphore_signal(barrier, inc=1, device_id={"head": 1 - my_head}, device_id_type=MESH)

    def local(src, dst, i):
        copy = pltpu.make_async_copy(src, dst, local_sem.at[i])
        copy.start()
        return copy

    latents_copy = local(latents_in, latents, 12)
    keys_copy = local(keys_in, keys, 13)
    cot_copy = local(cot.at[0], cot_buf, 1)
    w_copy = local(weight, w_buf, 0)
    values_copy = local(values_in, values, 14)
    my_share = pl.ds(pl.multiple_of(my_slide * share, 16), share)
    mask_own[...] = jnp.zeros_like(mask_own)
    for b in range(blocks):
        mask_own[pl.ds(b, 1), :] = jnp.full((1, 128), mask[0, b], jnp.int32)
    mask_all[side] = mask_own[...]

    sent = []

    def send(kind, d, src, dst):
        copy = pltpu.make_async_remote_copy(
            src_ref=src,
            dst_ref=dst,
            send_sem=send_sem.at[kind, d - 1],
            recv_sem=recv_sem.at[kind, d - 1],
            device_id={"seq": peer(d)},
            device_id_type=MESH,
        )
        copy.start()
        sent.append(copy)
        return copy

    far = [n // 2] + [d for d in range(n - 1, 0, -1) if d != n // 2]
    pl.semaphore_wait(barrier, n - 1 + slides - 1 + 1)
    mask_moves = [send(0, 1, mask_own, mask_all.at[side])]
    latents_copy.wait()
    own_q = local(latents.at[my_share, cols(side)], q_all.at[me, my_slide], 2)
    q_moves = [send(1, d, latents.at[my_share, cols_for(d)], q_all.at[me, my_slide]) for d in far]
    keys_copy.wait()
    own_k = local(keys.at[0, :, cols(side)], k_all.at[rows_of(side, tiles)], 3)
    k_moves = [send(2, 1, keys.at[0, :, cols_for(1)], k_all.at[rows_of(side, tiles)])]

    live_count = count[0]
    w_copy.wait()
    cot_copy.wait()
    own_row = lax.broadcasted_iota(jnp.int32, (rows, 1), 0) + me * rows
    projected = dot(cot_buf[...], w_buf[...], ((1,), (1,)))
    u_own[...] = jnp.where(own_row < live_count, projected, 0.0).astype(jnp.bfloat16)
    own_u = local(u_own.at[:, cols(side)], u_all.at[rows_of(me, rows)], 5)
    u_moves = [send(4, d, u_own.at[:, cols_for(d)], u_all.at[rows_of(me, rows)]) for d in far]

    lane = lax.broadcasted_iota(jnp.int32, (1, blk), 1) // HD

    def only(x, h):
        return jnp.where(lane == h, x, jnp.zeros_like(x))

    own_q.wait()
    for copy in q_moves:
        copy.wait_recv()
    share_moves = []
    for e in range(1, slides):
        copy = pltpu.make_async_remote_copy(
            src_ref=q_all.at[:, my_slide],
            dst_ref=q_all.at[:, my_slide],
            send_sem=share_send.at[e - 1],
            recv_sem=share_recv.at[e - 1],
            device_id={"slide": lax.rem(my_slide + e, slides)},
            device_id_type=MESH,
        )
        copy.start()
        share_moves.append(copy)
    own_k.wait()
    for copy in mask_moves + share_moves + k_moves:
        copy.wait_recv()
    values_copy.wait()
    own_v = local(values.at[0, :, cols(side)], v_all.at[rows_of(side, tiles)], 4)
    v_moves = [send(3, 1, values.at[0, :, cols_for(1)], v_all.at[rows_of(side, tiles)])]

    q_rows = q_all[...].reshape(all_rows, blk)

    tops = []
    totals = []
    for h in range(heads):
        query = only(q_rows, h)

        def score_step(i, top, h=h, query=query):
            scores = dot(k_all[rows_of(i, tiles), :], query, ((1,), (1,))) * factor
            for b in range(blocks):
                at = pl.ds(pl.multiple_of(i * tiles + b * BLOCK, BLOCK), BLOCK)
                score = scores[b * BLOCK : (b + 1) * BLOCK]
                valid = jnp.broadcast_to(mask_all[i][b : b + 1, :1], (1, all_rows)) > 0
                score = jnp.where(valid, score, masked_score)
                probs[h, at, :] = score
                top = jnp.maximum(top, jnp.max(score, axis=0, keepdims=True))
            return top

        top = lax.fori_loop(0, g, score_step, jnp.full((1, all_rows), masked_score, jnp.float32))

        tops.append(top)

        def exp_step(i, total, h=h, top=top):
            for b in range(blocks):
                at = pl.ds(pl.multiple_of(i * tiles + b * BLOCK, BLOCK), BLOCK)
                expos = jnp.exp(probs[h, at, :] - top)
                probs[h, at, :] = expos
                total = total + jnp.sum(expos, axis=0, keepdims=True)
            return total

        totals.append(lax.fori_loop(0, g, exp_step, jnp.zeros((1, all_rows), jnp.float32)))
    stats[...] = jnp.zeros_like(stats)
    for h in range(heads):
        stats[pl.ds(h, 1), :] = tops[h]
        stats[pl.ds(heads + h, 1), :] = totals[h]
    stat_moves = [send(9, d, stats, stats_in.at[d // g - 1]) for d in range(g, n, g)]
    for copy in stat_moves:
        copy.wait_recv()
    inverse = []
    for h in range(heads):
        other_tops = [stats_in[e, h : h + 1, :] for e in range(n // g - 1)]
        whole_top = functools.reduce(jnp.maximum, other_tops, tops[h])
        whole_total = totals[h] * jnp.exp(tops[h] - whole_top)
        for e, other in enumerate(other_tops):
            more = stats_in[e, heads + h : heads + h + 1, :]
            whole_total = whole_total + more * jnp.exp(other - whole_top)
        inverse.append(jnp.exp(tops[h] - whole_top) / whole_total)

    own_u.wait()
    for copy in u_moves:
        copy.wait_recv()
    u_rows = u_all[...]
    gv_moves = []
    for d in (1, 0):
        at = rows_of(lax.rem(peer(d), g), tiles)
        grad_v = None
        for h in range(heads):
            weights = probs[h, at, :] * inverse[h]
            probs[h, at, :] = weights
            more_v = dot(weights.astype(jnp.bfloat16), only(u_rows, h), ((1,), (0,)))
            grad_v = more_v if grad_v is None else grad_v + more_v
        gv[at, :] = grad_v.astype(jnp.bfloat16)
        if d:
            gv_moves.append(send(7, d, gv.at[at], grad_values.at[0, :, cols(side)]))
        else:
            own_gv = local(gv.at[at], grad_values.at[0, :, cols(side)], 8)

    own_v.wait()
    for copy in v_moves:
        copy.wait_recv()

    def attend_step(i, sums):
        at = rows_of(i, tiles)
        v_block = v_all[at, :]
        for h in range(heads):
            weights = probs[h, at, :].astype(jnp.bfloat16)
            sums = sums + dot(only(v_block, h), weights, ((0,), (0,)))
        return sums

    zero = jnp.zeros((blk, all_rows), jnp.float32)
    attended = lax.fori_loop(0, g, attend_step, zero)
    every_row = lax.broadcasted_iota(jnp.int32, (1, all_rows), 1)
    attended = jnp.where(every_row < live_count, attended, 0.0)
    attended_rows = attended.T.astype(jnp.bfloat16)
    att[...] = attended_rows
    own_att = local(att.at[rows_of(me, rows)], att_in.at[part, :, cols(side)], 6)
    att_moves = [send(5, d, att.at[rows_of(peer(d), rows)], att_in.at[part, :, cols(side)]) for d in far]

    product = u_rows.astype(jnp.float32).T * attended
    delta = [jnp.sum(product[h * HD : (h + 1) * HD], axis=0, keepdims=True) for h in range(heads)]
    deltas[...] = jnp.zeros_like(deltas)
    for h in range(heads):
        deltas[pl.ds(h, 1), :] = delta[h]
    delta_moves = [send(10, d, deltas, deltas_in.at[d // g - 1]) for d in range(g, n, g)]
    for e, copy in enumerate(delta_moves):
        copy.wait_recv()
        delta = [delta[h] + deltas_in[e, h : h + 1, :] for h in range(heads)]

    grad_q = zero
    gk_moves = []
    for d in (1, 0):
        at = rows_of(lax.rem(peer(d), g), tiles)
        v_block = v_all[at, :]
        k_block = k_all[at, :]
        grad_k = None
        for h in range(heads):
            query = only(q_rows, h)
            grad_prob = dot(v_block, only(u_rows, h), ((1,), (1,)))
            weights = probs[h, at, :]
            grad_score = (weights * (grad_prob - delta[h]) * factor).astype(jnp.bfloat16)
            more_k = dot(grad_score, query, ((1,), (0,)))
            grad_k = more_k if grad_k is None else grad_k + more_k
            grad_q = grad_q + dot(only(k_block, h), grad_score, ((0,), (0,)))
        gk[at, :] = grad_k.astype(jnp.bfloat16)
        if d:
            gk_moves.append(send(6, d, gk.at[at], grad_keys.at[0, :, cols(side)]))
        else:
            own_gk = local(gk.at[at], grad_keys.at[0, :, cols(side)], 7)

    grad_rows = grad_q.T
    gq[...] = grad_rows.astype(jnp.bfloat16)
    slide_moves = []
    for e in range(1, slides):
        copy = pltpu.make_async_remote_copy(
            src_ref=gq,
            dst_ref=gq_in.at[e - 1],
            send_sem=slide_send.at[e - 1],
            recv_sem=slide_recv.at[e - 1],
            device_id={"slide": lax.rem(my_slide + e, slides)},
            device_id_type=MESH,
        )
        copy.start()
        slide_moves.append(copy)

    own_att.wait()
    for copy in att_moves:
        copy.wait_recv()
    half = pooled.shape[2]
    mine = pl.ds(pl.multiple_of(my_head * half, 128), half)
    theirs = pl.ds(pl.multiple_of((1 - my_head) * half, 128), half)
    att_sum = att_in[0].astype(jnp.float32)
    for e in range(1, n // g):
        att_sum = att_sum + att_in[e].astype(jnp.float32)
    att_sum = att_sum.astype(jnp.bfloat16)
    part_out[...] = dot(att_sum, w_buf[:, theirs], ((1,), (0,))).astype(jnp.bfloat16)
    head_move = pltpu.make_async_remote_copy(
        src_ref=part_out,
        dst_ref=part_in,
        send_sem=head_send,
        recv_sem=head_recv,
        device_id={"head": 1 - my_head},
        device_id_type=MESH,
    )
    head_move.start()
    own_part = dot(att_sum, w_buf[:, mine], ((1,), (0,)))

    total = grad_rows
    for e, copy in enumerate(slide_moves):
        copy.wait_recv()
        total = total + gq_in[e].astype(jnp.float32)
    gq_sum[...] = total.astype(jnp.bfloat16)
    own_gl = local(gq_sum.at[rows_of(me, rows)], gl_in.at[part, :, cols(side)], 9)
    gl_moves = [send(8, d, gq_sum.at[rows_of(peer(d), rows)], gl_in.at[part, :, cols(side)]) for d in far]

    head_move.wait_recv()
    pooled[0] = (own_part + part_in[...].astype(jnp.float32)).astype(jnp.bfloat16)

    own_gl.wait()
    for copy in gl_moves:
        copy.wait_recv()
    gl_sum = gl_in[0].astype(jnp.float32)
    for e in range(1, n // g):
        gl_sum = gl_sum + gl_in[e].astype(jnp.float32)
    grad_latents[...] = gl_sum
    own_gk.wait()
    own_gv.wait()
    for copy in gk_moves + gv_moves:
        copy.wait_recv()
    for copy in sent + slide_moves + share_moves + [head_move]:
        copy.wait_send()


def finish_kernel(count, *refs):
    sems = refs[-1]
    copies = [pltpu.make_async_copy(refs[i], refs[count + i], sems.at[i]) for i in range(count)]
    for copy in copies:
        copy.start()
    for copy in copies:
        copy.wait()


def swapped_body(latents, tile_keys, tile_values, tile_mask, latent_counts, out_weight, cotangent):
    n = lax.axis_size("seq")
    slides = lax.axis_size("slide")
    rows, width = latents.shape
    tiles = tile_keys.shape[1]
    depth = out_weight.shape[1]
    g = PAIR
    blk = width // g
    heads = blk // HD
    half = depth // 2
    bf16 = jnp.bfloat16
    anywhere = pl.BlockSpec(memory_space=pl.ANY)
    scalars = pl.BlockSpec(memory_space=pltpu.SMEM)
    dma = pltpu.SemaphoreType.DMA
    flops = 2 * heads * 6 * n * rows * g * tiles * HD + 4 * rows * width * depth
    results = pl.pallas_call(
        functools.partial(swap_kernel, n, slides),
        out_shape=(
            pltpu.VMEM((1, rows, half), bf16),
            pltpu.VMEM((rows, width), jnp.float32),
            pltpu.VMEM(tile_keys.shape, bf16),
            pltpu.VMEM(tile_values.shape, bf16),
        ),
        in_specs=[anywhere, anywhere, anywhere, scalars, scalars, anywhere, anywhere],
        out_specs=(pl.BlockSpec(memory_space=pltpu.VMEM),) * 4,
        scratch_shapes=[
            pltpu.VMEM((n, slides, rows // slides, blk), bf16),
            pltpu.VMEM((g * tiles, blk), bf16),
            pltpu.VMEM((g * tiles, blk), bf16),
            pltpu.VMEM((n * rows, blk), bf16),
            pltpu.VMEM((8 * pl.cdiv(tiles // BLOCK, 8), 128), jnp.int32),
            pltpu.VMEM((g, 8 * pl.cdiv(tiles // BLOCK, 8), 128), jnp.int32),
            pltpu.VMEM((width, depth), bf16),
            pltpu.VMEM((rows, depth), bf16),
            pltpu.VMEM((rows, width), bf16),
            pltpu.VMEM((heads, g * tiles, n * rows), jnp.float32),
            pltpu.VMEM((n * rows, blk), bf16),
            pltpu.VMEM((n // g, rows, width), bf16),
            pltpu.VMEM((rows, half), bf16),
            pltpu.VMEM((rows, half), bf16),
            pltpu.VMEM((g * tiles, blk), bf16),
            pltpu.VMEM((g * tiles, blk), bf16),
            pltpu.VMEM((n * rows, blk), bf16),
            pltpu.VMEM((slides - 1, n * rows, blk), bf16),
            pltpu.VMEM((n * rows, blk), bf16),
            pltpu.VMEM((n // g, rows, width), bf16),
            pltpu.VMEM(latents.shape, bf16),
            pltpu.VMEM(tile_keys.shape, bf16),
            pltpu.VMEM(tile_values.shape, bf16),
            pltpu.VMEM((8 * pl.cdiv(2 * heads, 8), n * rows), jnp.float32),
            pltpu.VMEM((n // g - 1, 8 * pl.cdiv(2 * heads, 8), n * rows), jnp.float32),
            pltpu.VMEM((8 * pl.cdiv(heads, 8), n * rows), jnp.float32),
            pltpu.VMEM((n // g - 1, 8 * pl.cdiv(heads, 8), n * rows), jnp.float32),
            dma((15,)),
            dma((11, n - 1)),
            dma((11, n - 1)),
            dma((slides - 1,)),
            dma((slides - 1,)),
            dma((slides - 1,)),
            dma((slides - 1,)),
            dma,
            dma,
        ],
        compiler_params=pltpu.CompilerParams(
            collective_id=0, has_side_effects=True, vmem_limit_bytes=60 * 1024 * 1024
        ),
        cost_estimate=pl.CostEstimate(
            flops=flops, bytes_accessed=8 * rows * depth * 2, transcendentals=heads * n * rows * g * tiles
        ),
    )(latents, tile_keys, tile_values, tile_mask, latent_counts, out_weight, cotangent)
    return pl.pallas_call(
        functools.partial(finish_kernel, len(results)),
        out_shape=tuple(jax.ShapeDtypeStruct(x.shape, x.dtype) for x in results),
        in_specs=[anywhere] * len(results),
        out_specs=(anywhere,) * len(results),
        scratch_shapes=[dma((len(results),))],
        compiler_params=pltpu.CompilerParams(vmem_limit_bytes=4 * 1024 * 1024),
    )(*results)


def body(latents, tile_keys, tile_values, tile_mask, latent_counts, out_weight, cotangent):
    local_rows = latents.shape[0]
    local_width = latents.shape[1]
    head_count = local_width // HD
    factor = HD ** (-0.5)
    queries = lax.all_gather(latents, "seq", axis=0, tiled=True)
    total_rows = queries.shape[0]
    first_row = lax.axis_index("seq") * local_rows
    every_row = lax.broadcasted_iota(jnp.int32, (total_rows, 1), 0)
    own_row = lax.broadcasted_iota(jnp.int32, (local_rows, 1), 0) + first_row
    tile_count = tile_keys.shape[1]
    key_block = tile_keys[0]
    value_block = tile_values[0]
    valid_tiles = jnp.broadcast_to(tile_mask[0][:, None] > 0, (tile_count // BLOCK, BLOCK)).reshape(
        1, tile_count
    )
    live_count = latent_counts[0]
    score_list = []
    for which_head in range(head_count):
        columns = slice(which_head * HD, (which_head + 1) * HD)
        raw_scores = (
            jnp.einsum(
                "qc,tc->qt",
                queries[:, columns],
                key_block[:, columns],
                preferred_element_type=jnp.float32,
            )
            * factor
        )
        score_list.append(jnp.where(valid_tiles, raw_scores, masked_score))
    local_top = jnp.stack([jnp.max(scored, axis=1) for scored in score_list], axis=1)
    row_top = lax.pmax(local_top, "seq")
    expo_list = []
    weighted_list = []
    total_list = []
    for which_head in range(head_count):
        columns = slice(which_head * HD, (which_head + 1) * HD)
        expos = jnp.where(
            valid_tiles,
            jnp.exp(score_list[which_head] - row_top[:, which_head : which_head + 1]),
            0.0,
        )
        expo_list.append(expos)
        total_list.append(jnp.sum(expos, axis=1))
        weighted_list.append(
            jnp.dot(
                expos.astype(jnp.bfloat16),
                value_block[:, columns],
                preferred_element_type=jnp.float32,
            )
        )
    partial_sums = jnp.concatenate(weighted_list, axis=1)
    partial_totals = jnp.stack(total_list, axis=1)
    weighted, totals = lax.psum((partial_sums, partial_totals), "seq")
    span = weighted.shape[0]
    attended = jnp.where(
        every_row < live_count,
        (weighted.reshape(span, head_count, HD) / totals[:, :, None]).reshape(span, local_width),
        0.0,
    ).astype(jnp.bfloat16)
    own_attended = lax.dynamic_slice_in_dim(attended, first_row, local_rows, 0)
    pooled_part = jnp.dot(own_attended, out_weight, preferred_element_type=jnp.float32)
    pooled_parts = [
        lax.psum_scatter(pooled_part.astype(jnp.bfloat16), "head", scatter_dimension=1, tiled=True)
    ]
    projected = jnp.einsum(
        "rd,cd->rc", cotangent[0], out_weight, preferred_element_type=jnp.float32
    )
    upstream = jnp.where(own_row < live_count, projected, 0.0).astype(jnp.bfloat16)
    upstream_all = lax.all_gather(upstream, "seq", axis=0, tiled=True)
    row_delta = jnp.sum(
        (upstream_all.astype(jnp.float32) * attended.astype(jnp.float32)).reshape(
            total_rows, head_count, HD
        ),
        axis=2,
    )
    query_list = []
    key_list = []
    value_list = []
    for which_head in range(head_count):
        columns = slice(which_head * HD, (which_head + 1) * HD)
        up_head = upstream_all[:, columns]
        weights = expo_list[which_head] / totals[:, which_head : which_head + 1]
        value_list.append(
            jnp.einsum(
                "qt,qc->tc",
                weights.astype(jnp.bfloat16),
                up_head,
                preferred_element_type=jnp.float32,
            )
        )
        grad_prob = jnp.einsum(
            "qc,tc->qt", up_head, value_block[:, columns], preferred_element_type=jnp.float32
        )
        grad_score = (
            weights * (grad_prob - row_delta[:, which_head : which_head + 1]) * factor
        ).astype(jnp.bfloat16)
        query_list.append(
            jnp.dot(grad_score, key_block[:, columns], preferred_element_type=jnp.float32)
        )
        key_list.append(
            jnp.einsum(
                "qt,qc->tc", grad_score, queries[:, columns], preferred_element_type=jnp.float32
            )
        )
    grad_rows = jnp.concatenate(query_list, axis=1)
    key_grads = [jnp.concatenate(key_list, axis=1).astype(jnp.bfloat16)]
    value_grads = [jnp.concatenate(value_list, axis=1).astype(jnp.bfloat16)]
    own_grad = lax.psum_scatter(
        grad_rows.astype(jnp.bfloat16), "seq", scatter_dimension=0, tiled=True
    )
    grad_latents = lax.psum(own_grad, "slide").astype(jnp.float32)
    return (
        jnp.stack(pooled_parts, axis=0),
        grad_latents,
        jnp.stack(key_grads, axis=0),
        jnp.stack(value_grads, axis=0),
    )


def solution(mesh):
    placed = (
        P(("groups", "seq"), "head"),
        P(("groups", "slide"), "seq", "head"),
        P(("groups", "slide"), "seq", "head"),
        P(("groups", "slide"), "seq"),
        P(("groups", "slide")),
        P("head", None),
        P(("groups", "slide"), "seq", None),
    )
    block_width = 128 * PAIR
    swapped = mesh.shape["seq"] in (4, 8) and mesh.shape["slide"] > 1 and mesh.shape["head"] == 2

    def chosen(latents, *others):
        by_heads = swapped and latents.shape[1] % block_width == 0
        by_heads = by_heads and latents.shape[0] % 128 == 0
        by_heads = by_heads and latents.shape[0] % (16 * mesh.shape["slide"]) == 0 and others[0].shape[1] % BLOCK == 0
        return (swapped_body if by_heads else body)(latents, *others)

    return jax.shard_map(
        chosen,
        mesh=mesh,
        in_specs=placed,
        out_specs=(
            P(("groups", "slide"), "seq", "head"),
            P(("groups", "seq"), "head"),
            P(("groups", "slide"), "seq", "head"),
            P(("groups", "slide"), "seq", "head"),
        ),
        check_vma=False,
    )
```

```python
import functools

import jax
import jax.numpy as jnp
from jax import lax
from jax.experimental import pallas as pl
from jax.experimental.pallas import tpu as pltpu
from jax.sharding import PartitionSpec as P

HD = 64
BLOCK = 128


masked_score = -1e30


MESH = pl.DeviceIdType.MESH


def dot(a, b, dims):
    return lax.dot_general(a, b, (dims, ((), ())), preferred_element_type=jnp.float32)


def swap_kernel(
    n,
    slides,
    latents_in,
    keys_in,
    values_in,
    mask,
    count,
    weight,
    cot,
    pooled,
    grad_latents,
    grad_keys,
    grad_values,
    q_all,
    k_all,
    v_all,
    u_all,
    mask_own,
    mask_all,
    w_buf,
    cot_buf,
    u_own,
    probs,
    grad_scores,
    att,
    att_in,
    part_out,
    part_in,
    gk,
    gv,
    gq,
    gq_in,
    gq_sum,
    gl_in,
    latents,
    keys,
    values,
    local_sem,
    send_sem,
    recv_sem,
    slide_send,
    slide_recv,
    share_send,
    share_recv,
    head_send,
    head_recv,
):
    me = lax.axis_index("seq")
    my_head = lax.axis_index("head")
    my_slide = lax.axis_index("slide")
    rows = latents.shape[0]
    tiles = keys.shape[1]
    blk = k_all.shape[1]
    share = rows // slides
    heads = blk // HD
    width = latents.shape[1]
    all_rows = n * rows
    blocks = tiles // BLOCK
    factor = HD ** (-0.5)

    def cols(j):
        return pl.ds(pl.multiple_of(j * blk, 128), blk)

    def rows_of(j, size):
        return pl.ds(pl.multiple_of(j * size, 128), size)

    def peer(d):
        other, bit = me, 1
        while bit < n:
            if d & bit:
                other = other + bit - 2 * bit * lax.rem(lax.div(me, bit), 2)
            bit *= 2
        return other

    barrier = pltpu.get_barrier_semaphore()
    for d in range(1, n):
        pl.semaphore_signal(barrier, inc=1, device_id={"seq": peer(d)}, device_id_type=MESH)
    for e in range(1, slides):
        other = lax.rem(my_slide + e, slides)
        pl.semaphore_signal(barrier, inc=1, device_id={"slide": other}, device_id_type=MESH)
    pl.semaphore_signal(barrier, inc=1, device_id={"head": 1 - my_head}, device_id_type=MESH)

    def local(src, dst, i):
        copy = pltpu.make_async_copy(src, dst, local_sem.at[i])
        copy.start()
        return copy

    latents_copy = local(latents_in, latents, 12)
    keys_copy = local(keys_in, keys, 13)
    cot_copy = local(cot.at[0], cot_buf, 1)
    w_copy = local(weight, w_buf, 0)
    values_copy = local(values_in, values, 14)
    my_share = pl.ds(pl.multiple_of(my_slide * share, 16), share)
    mask_own[...] = jnp.zeros_like(mask_own)
    for b in range(blocks):
        mask_own[pl.ds(b, 1), :] = jnp.full((1, 128), mask[0, b], jnp.int32)
    mask_all[me] = mask_own[...]

    sent = []

    def send(kind, d, src, dst):
        copy = pltpu.make_async_remote_copy(
            src_ref=src,
            dst_ref=dst,
            send_sem=send_sem.at[kind, d - 1],
            recv_sem=recv_sem.at[kind, d - 1],
            device_id={"seq": peer(d)},
            device_id_type=MESH,
        )
        copy.start()
        sent.append(copy)
        return copy

    far = [n // 2] + [d for d in range(n - 1, 0, -1) if d != n // 2]
    pl.semaphore_wait(barrier, n - 1 + slides - 1 + 1)
    mask_moves = [send(0, d, mask_own, mask_all.at[me]) for d in far]
    latents_copy.wait()
    own_q = local(latents.at[my_share, cols(me)], q_all.at[me, my_slide], 2)
    q_moves = [send(1, d, latents.at[my_share, cols(peer(d))], q_all.at[me, my_slide]) for d in far]
    keys_copy.wait()
    own_k = local(keys.at[0, :, cols(me)], k_all.at[rows_of(me, tiles)], 3)
    k_moves = [send(2, d, keys.at[0, :, cols(peer(d))], k_all.at[rows_of(me, tiles)]) for d in far]

    live_count = count[0]
    w_copy.wait()
    cot_copy.wait()
    own_row = lax.broadcasted_iota(jnp.int32, (rows, 1), 0) + me * rows
    projected = dot(cot_buf[...], w_buf[...], ((1,), (1,)))
    u_own[...] = jnp.where(own_row < live_count, projected, 0.0).astype(jnp.bfloat16)
    own_u = local(u_own.at[:, cols(me)], u_all.at[rows_of(me, rows)], 5)
    u_moves = [send(4, d, u_own.at[:, cols(peer(d))], u_all.at[rows_of(me, rows)]) for d in far]

    lane = lax.broadcasted_iota(jnp.int32, (1, blk), 1) // HD

    def only(x, h):
        return jnp.where(lane == h, x, jnp.zeros_like(x))

    own_q.wait()
    for copy in q_moves:
        copy.wait_recv()
    share_moves = []
    for e in range(1, slides):
        copy = pltpu.make_async_remote_copy(
            src_ref=q_all.at[:, my_slide],
            dst_ref=q_all.at[:, my_slide],
            send_sem=share_send.at[e - 1],
            recv_sem=share_recv.at[e - 1],
            device_id={"slide": lax.rem(my_slide + e, slides)},
            device_id_type=MESH,
        )
        copy.start()
        share_moves.append(copy)
    own_k.wait()
    for copy in mask_moves + share_moves + k_moves:
        copy.wait_recv()
    values_copy.wait()
    own_v = local(values.at[0, :, cols(me)], v_all.at[rows_of(me, tiles)], 4)
    v_moves = [send(3, d, values.at[0, :, cols(peer(d))], v_all.at[rows_of(me, tiles)]) for d in far]

    q_rows = q_all[...].reshape(all_rows, blk)

    tops = []
    totals = []
    for h in range(heads):
        query = only(q_rows, h)

        def score_step(i, top, h=h, query=query):
            scores = dot(k_all[rows_of(i, tiles), :], query, ((1,), (1,))) * factor
            for b in range(blocks):
                at = pl.ds(pl.multiple_of(i * tiles + b * BLOCK, BLOCK), BLOCK)
                score = scores[b * BLOCK : (b + 1) * BLOCK]
                valid = jnp.broadcast_to(mask_all[i][b : b + 1, :1], (1, all_rows)) > 0
                score = jnp.where(valid, score, masked_score)
                probs[h, at, :] = score
                top = jnp.maximum(top, jnp.max(score, axis=0, keepdims=True))
            return top

        top = lax.fori_loop(0, n, score_step, jnp.full((1, all_rows), masked_score, jnp.float32))

        def exp_step(i, total, h=h, top=top):
            for b in range(blocks):
                at = pl.ds(pl.multiple_of(i * tiles + b * BLOCK, BLOCK), BLOCK)
                expos = jnp.exp(probs[h, at, :] - top)
                probs[h, at, :] = expos
                total = total + jnp.sum(expos, axis=0, keepdims=True)
            return total

        totals.append(lax.fori_loop(0, n, exp_step, jnp.zeros((1, all_rows), jnp.float32)))
    inverse = [1.0 / total for total in totals]

    own_u.wait()
    for copy in u_moves:
        copy.wait_recv()
    u_rows = u_all[...]
    gv_moves = []
    for d in far + [0]:
        j = peer(d)
        at = rows_of(j, tiles)
        grad_v = None
        for h in range(heads):
            weights = probs[h, at, :] * inverse[h]
            probs[h, at, :] = weights
            more_v = dot(weights.astype(jnp.bfloat16), only(u_rows, h), ((1,), (0,)))
            grad_v = more_v if grad_v is None else grad_v + more_v
        gv[at, :] = grad_v.astype(jnp.bfloat16)
        if d:
            gv_moves.append(send(7, d, gv.at[at], grad_values.at[0, :, cols(me)]))
        else:
            own_gv = local(gv.at[at], grad_values.at[0, :, cols(me)], 8)

    own_v.wait()
    for copy in v_moves:
        copy.wait_recv()

    def attend_step(i, sums):
        at = rows_of(i, tiles)
        v_block = v_all[at, :]
        for h in range(heads):
            weights = probs[h, at, :].astype(jnp.bfloat16)
            sums = sums + dot(only(v_block, h), weights, ((0,), (0,)))
        return sums

    zero = jnp.zeros((blk, all_rows), jnp.float32)
    attended = lax.fori_loop(0, n, attend_step, zero)
    every_row = lax.broadcasted_iota(jnp.int32, (1, all_rows), 1)
    attended = jnp.where(every_row < live_count, attended, 0.0)
    attended_rows = attended.T.astype(jnp.bfloat16)
    att[...] = attended_rows
    own_att = local(att.at[rows_of(me, rows)], att_in.at[:, cols(me)], 6)
    att_moves = [send(5, d, att.at[rows_of(peer(d), rows)], att_in.at[:, cols(me)]) for d in far]

    product = u_rows.astype(jnp.float32) * attended_rows.astype(jnp.float32)
    product = product.T
    delta = [jnp.sum(product[h * HD : (h + 1) * HD], axis=0, keepdims=True) for h in range(heads)]

    grad_q = zero
    for d in far + [0]:
        at = rows_of(peer(d), tiles)
        v_block = v_all[at, :]
        k_block = k_all[at, :]
        for h in range(heads):
            grad_prob = dot(v_block, only(u_rows, h), ((1,), (1,)))
            grad_score = (probs[h, at, :] * (grad_prob - delta[h]) * factor).astype(jnp.bfloat16)
            grad_scores[h, at, :] = grad_score
            grad_q = grad_q + dot(only(k_block, h), grad_score, ((0,), (0,)))

    grad_rows = grad_q.T
    gq[...] = grad_rows.astype(jnp.bfloat16)
    slide_moves = []
    for e in range(1, slides):
        copy = pltpu.make_async_remote_copy(
            src_ref=gq,
            dst_ref=gq_in.at[e - 1],
            send_sem=slide_send.at[e - 1],
            recv_sem=slide_recv.at[e - 1],
            device_id={"slide": lax.rem(my_slide + e, slides)},
            device_id_type=MESH,
        )
        copy.start()
        slide_moves.append(copy)

    gk_moves = []
    for d in far + [0]:
        at = rows_of(peer(d), tiles)
        grad_k = dot(grad_scores[0, at, :], only(q_rows, 0), ((1,), (0,)))
        for h in range(1, heads):
            grad_k = grad_k + dot(grad_scores[h, at, :], only(q_rows, h), ((1,), (0,)))
        gk[at, :] = grad_k.astype(jnp.bfloat16)
        if d:
            gk_moves.append(send(6, d, gk.at[at], grad_keys.at[0, :, cols(me)]))
        else:
            own_gk = local(gk.at[at], grad_keys.at[0, :, cols(me)], 7)

    total = grad_rows
    for e, copy in enumerate(slide_moves):
        copy.wait_recv()
        total = total + gq_in[e].astype(jnp.float32)
    gq_sum[...] = total.astype(jnp.bfloat16)
    own_gl = local(gq_sum.at[rows_of(me, rows)], gl_in.at[:, cols(me)], 9)
    gl_moves = [send(8, d, gq_sum.at[rows_of(peer(d), rows)], gl_in.at[:, cols(me)]) for d in far]

    own_att.wait()
    for copy in att_moves:
        copy.wait_recv()
    half = pooled.shape[2]
    mine = pl.ds(pl.multiple_of(my_head * half, 128), half)
    theirs = pl.ds(pl.multiple_of((1 - my_head) * half, 128), half)
    part_out[...] = dot(att_in[...], w_buf[:, theirs], ((1,), (0,))).astype(jnp.bfloat16)
    head_move = pltpu.make_async_remote_copy(
        src_ref=part_out,
        dst_ref=part_in,
        send_sem=head_send,
        recv_sem=head_recv,
        device_id={"head": 1 - my_head},
        device_id_type=MESH,
    )
    head_move.start()
    own_part = dot(att_in[...], w_buf[:, mine], ((1,), (0,)))

    head_move.wait_recv()
    pooled[0] = (own_part + part_in[...].astype(jnp.float32)).astype(jnp.bfloat16)

    own_gl.wait()
    for copy in gl_moves:
        copy.wait_recv()
    grad_latents[...] = gl_in[...].astype(jnp.float32)
    own_gk.wait()
    own_gv.wait()
    for copy in gk_moves + gv_moves:
        copy.wait_recv()
    for copy in sent + slide_moves + share_moves + [head_move]:
        copy.wait_send()


def finish_kernel(count, *refs):
    sems = refs[-1]
    copies = [pltpu.make_async_copy(refs[i], refs[count + i], sems.at[i]) for i in range(count)]
    for copy in copies:
        copy.start()
    for copy in copies:
        copy.wait()


def swapped_body(latents, tile_keys, tile_values, tile_mask, latent_counts, out_weight, cotangent):
    n = lax.axis_size("seq")
    slides = lax.axis_size("slide")
    rows, width = latents.shape
    tiles = tile_keys.shape[1]
    depth = out_weight.shape[1]
    blk = width // n
    heads = blk // HD
    half = depth // 2
    bf16 = jnp.bfloat16
    anywhere = pl.BlockSpec(memory_space=pl.ANY)
    scalars = pl.BlockSpec(memory_space=pltpu.SMEM)
    dma = pltpu.SemaphoreType.DMA
    flops = 2 * heads * 6 * n * rows * n * tiles * HD + 4 * rows * width * depth
    results = pl.pallas_call(
        functools.partial(swap_kernel, n, slides),
        out_shape=(
            pltpu.VMEM((1, rows, half), bf16),
            pltpu.VMEM((rows, width), jnp.float32),
            pltpu.VMEM(tile_keys.shape, bf16),
            pltpu.VMEM(tile_values.shape, bf16),
        ),
        in_specs=[anywhere, anywhere, anywhere, scalars, scalars, anywhere, anywhere],
        out_specs=(pl.BlockSpec(memory_space=pltpu.VMEM),) * 4,
        scratch_shapes=[
            pltpu.VMEM((n, slides, rows // slides, blk), bf16),
            pltpu.VMEM((n * tiles, blk), bf16),
            pltpu.VMEM((n * tiles, blk), bf16),
            pltpu.VMEM((n * rows, blk), bf16),
            pltpu.VMEM((8 * pl.cdiv(tiles // BLOCK, 8), 128), jnp.int32),
            pltpu.VMEM((n, 8 * pl.cdiv(tiles // BLOCK, 8), 128), jnp.int32),
            pltpu.VMEM((width, depth), bf16),
            pltpu.VMEM((rows, depth), bf16),
            pltpu.VMEM((rows, width), bf16),
            pltpu.VMEM((heads, n * tiles, n * rows), jnp.float32),
            pltpu.VMEM((heads, n * tiles, n * rows), bf16),
            pltpu.VMEM((n * rows, blk), bf16),
            pltpu.VMEM((rows, width), bf16),
            pltpu.VMEM((rows, half), bf16),
            pltpu.VMEM((rows, half), bf16),
            pltpu.VMEM((n * tiles, blk), bf16),
            pltpu.VMEM((n * tiles, blk), bf16),
            pltpu.VMEM((n * rows, blk), bf16),
            pltpu.VMEM((slides - 1, n * rows, blk), bf16),
            pltpu.VMEM((n * rows, blk), bf16),
            pltpu.VMEM((rows, width), bf16),
            pltpu.VMEM(latents.shape, bf16),
            pltpu.VMEM(tile_keys.shape, bf16),
            pltpu.VMEM(tile_values.shape, bf16),
            dma((15,)),
            dma((9, n - 1)),
            dma((9, n - 1)),
            dma((slides - 1,)),
            dma((slides - 1,)),
            dma((slides - 1,)),
            dma((slides - 1,)),
            dma,
            dma,
        ],
        compiler_params=pltpu.CompilerParams(
            collective_id=0, has_side_effects=True, vmem_limit_bytes=60 * 1024 * 1024
        ),
        cost_estimate=pl.CostEstimate(
            flops=flops, bytes_accessed=8 * rows * depth * 2, transcendentals=heads * n * rows * n * tiles
        ),
    )(latents, tile_keys, tile_values, tile_mask, latent_counts, out_weight, cotangent)
    return pl.pallas_call(
        functools.partial(finish_kernel, len(results)),
        out_shape=tuple(jax.ShapeDtypeStruct(x.shape, x.dtype) for x in results),
        in_specs=[anywhere] * len(results),
        out_specs=(anywhere,) * len(results),
        scratch_shapes=[dma((len(results),))],
        compiler_params=pltpu.CompilerParams(vmem_limit_bytes=4 * 1024 * 1024),
    )(*results)


def body(latents, tile_keys, tile_values, tile_mask, latent_counts, out_weight, cotangent):
    local_rows = latents.shape[0]
    local_width = latents.shape[1]
    head_count = local_width // HD
    factor = HD ** (-0.5)
    queries = lax.all_gather(latents, "seq", axis=0, tiled=True)
    total_rows = queries.shape[0]
    first_row = lax.axis_index("seq") * local_rows
    every_row = lax.broadcasted_iota(jnp.int32, (total_rows, 1), 0)
    own_row = lax.broadcasted_iota(jnp.int32, (local_rows, 1), 0) + first_row
    tile_count = tile_keys.shape[1]
    key_block = tile_keys[0]
    value_block = tile_values[0]
    valid_tiles = jnp.broadcast_to(tile_mask[0][:, None] > 0, (tile_count // BLOCK, BLOCK)).reshape(
        1, tile_count
    )
    live_count = latent_counts[0]
    score_list = []
    for which_head in range(head_count):
        columns = slice(which_head * HD, (which_head + 1) * HD)
        raw_scores = (
            jnp.einsum(
                "qc,tc->qt",
                queries[:, columns],
                key_block[:, columns],
                preferred_element_type=jnp.float32,
            )
            * factor
        )
        score_list.append(jnp.where(valid_tiles, raw_scores, masked_score))
    local_top = jnp.stack([jnp.max(scored, axis=1) for scored in score_list], axis=1)
    row_top = lax.pmax(local_top, "seq")
    expo_list = []
    weighted_list = []
    total_list = []
    for which_head in range(head_count):
        columns = slice(which_head * HD, (which_head + 1) * HD)
        expos = jnp.where(
            valid_tiles,
            jnp.exp(score_list[which_head] - row_top[:, which_head : which_head + 1]),
            0.0,
        )
        expo_list.append(expos)
        total_list.append(jnp.sum(expos, axis=1))
        weighted_list.append(
            jnp.dot(
                expos.astype(jnp.bfloat16),
                value_block[:, columns],
                preferred_element_type=jnp.float32,
            )
        )
    partial_sums = jnp.concatenate(weighted_list, axis=1)
    partial_totals = jnp.stack(total_list, axis=1)
    weighted, totals = lax.psum((partial_sums, partial_totals), "seq")
    span = weighted.shape[0]
    attended = jnp.where(
        every_row < live_count,
        (weighted.reshape(span, head_count, HD) / totals[:, :, None]).reshape(span, local_width),
        0.0,
    ).astype(jnp.bfloat16)
    own_attended = lax.dynamic_slice_in_dim(attended, first_row, local_rows, 0)
    pooled_part = jnp.dot(own_attended, out_weight, preferred_element_type=jnp.float32)
    pooled_parts = [
        lax.psum_scatter(pooled_part.astype(jnp.bfloat16), "head", scatter_dimension=1, tiled=True)
    ]
    projected = jnp.einsum(
        "rd,cd->rc", cotangent[0], out_weight, preferred_element_type=jnp.float32
    )
    upstream = jnp.where(own_row < live_count, projected, 0.0).astype(jnp.bfloat16)
    upstream_all = lax.all_gather(upstream, "seq", axis=0, tiled=True)
    row_delta = jnp.sum(
        (upstream_all.astype(jnp.float32) * attended.astype(jnp.float32)).reshape(
            total_rows, head_count, HD
        ),
        axis=2,
    )
    query_list = []
    key_list = []
    value_list = []
    for which_head in range(head_count):
        columns = slice(which_head * HD, (which_head + 1) * HD)
        up_head = upstream_all[:, columns]
        weights = expo_list[which_head] / totals[:, which_head : which_head + 1]
        value_list.append(
            jnp.einsum(
                "qt,qc->tc",
                weights.astype(jnp.bfloat16),
                up_head,
                preferred_element_type=jnp.float32,
            )
        )
        grad_prob = jnp.einsum(
            "qc,tc->qt", up_head, value_block[:, columns], preferred_element_type=jnp.float32
        )
        grad_score = (
            weights * (grad_prob - row_delta[:, which_head : which_head + 1]) * factor
        ).astype(jnp.bfloat16)
        query_list.append(
            jnp.dot(grad_score, key_block[:, columns], preferred_element_type=jnp.float32)
        )
        key_list.append(
            jnp.einsum(
                "qt,qc->tc", grad_score, queries[:, columns], preferred_element_type=jnp.float32
            )
        )
    grad_rows = jnp.concatenate(query_list, axis=1)
    key_grads = [jnp.concatenate(key_list, axis=1).astype(jnp.bfloat16)]
    value_grads = [jnp.concatenate(value_list, axis=1).astype(jnp.bfloat16)]
    own_grad = lax.psum_scatter(
        grad_rows.astype(jnp.bfloat16), "seq", scatter_dimension=0, tiled=True
    )
    grad_latents = lax.psum(own_grad, "slide").astype(jnp.float32)
    return (
        jnp.stack(pooled_parts, axis=0),
        grad_latents,
        jnp.stack(key_grads, axis=0),
        jnp.stack(value_grads, axis=0),
    )


def solution(mesh):
    placed = (
        P(("groups", "seq"), "head"),
        P(("groups", "slide"), "seq", "head"),
        P(("groups", "slide"), "seq", "head"),
        P(("groups", "slide"), "seq"),
        P(("groups", "slide")),
        P("head", None),
        P(("groups", "slide"), "seq", None),
    )
    block_width = 128 * mesh.shape["seq"]
    swapped = mesh.shape["seq"] in (2, 4, 8) and mesh.shape["slide"] > 1 and mesh.shape["head"] == 2

    def chosen(latents, *others):
        by_heads = swapped and latents.shape[1] % block_width == 0
        by_heads = by_heads and latents.shape[0] % 128 == 0
        by_heads = by_heads and latents.shape[0] % (16 * mesh.shape["slide"]) == 0 and others[0].shape[1] % BLOCK == 0
        return (swapped_body if by_heads else body)(latents, *others)

    return jax.shard_map(
        chosen,
        mesh=mesh,
        in_specs=placed,
        out_specs=(
            P(("groups", "slide"), "seq", "head"),
            P(("groups", "seq"), "head"),
            P(("groups", "slide"), "seq", "head"),
            P(("groups", "slide"), "seq", "head"),
        ),
        check_vma=False,
    )
```
